256 devices in a mesh: dp: 8 (over y, x_hi), tensor: 32 (over z, x_lo, core).
Axes of the slice: x: 4 (x_hi: 2, x_lo: 2; x = x_hi * 2 + x_lo), y: 4, z: 8, core: 2. Of those that a mesh axis runs over, the one named last changes fastest.
Arguments:
- hidden_in: bfloat16 [4096, 14848], P(('dp', 'tensor')), may hold values from -6 to 6
- norm_gain: bfloat16 [14848], replicated, may hold values from 0.5 to 1.5
- query_weight: bfloat16 [14848, 8192], P('dp', 'tensor'), may hold values from -0.046875 to 0.046875
- probe: bfloat16 [14848, 8192], P('dp', 'tensor'), may hold values from -0.046875 to 0.046875
- key_values: bfloat16 [4096, 1024], P(('dp', 'tensor')), may hold values from -6 to 6
- readout: bfloat16 [4096, 8192], P('dp', 'tensor'), may hold values from -0.0625 to 0.0625
- lengths: int32 [16, 2], P('dp'), may hold values from 32 to 128
- ref_margin: float32 [16], P('dp'), may hold values from -6 to 6
Outputs:
- hvp: float32 [14848, 8192], P('dp', 'tensor')
The draws below stay inside these ranges and needn't reach their ends.
All inputs are finite; a program needn't handle non-finite values.
Results may differ from the reference program's by a relative error of at most 0.04.
Values may be sent and summed in bfloat16 or wider, within the bound.
No kernel may reach another device: no remote copies, remote signals or barrier semaphores. Data moves between devices by JAX's collectives and lax.ppermute only.
A program may use at most 128 MiB of HBM per device.

```python
import jax
import jax.numpy as jnp
from jax import lax

D = 14848
HD = 64
KVH = 8
SEQ_LEN = 128
H = 128
PAIRS = 16
ROWS = 4096
N_DP = 8


def draw_lengths(key, part):
    key = jax.random.fold_in(key, 11)
    values = jax.random.randint(key, (PAIRS, 2), SEQ_LEN // 4, SEQ_LEN + 1, dtype=jnp.int32)
    values = values.at[0, 0].set(SEQ_LEN)
    values = values.at[0, 1].set(SEQ_LEN // 4)
    return values


def block_scale(stream_key, dims, shards, low, high):
    def one(dim, shards_of):
        draws = jax.random.uniform(jax.random.fold_in(jax.random.fold_in(stream_key, 6), dim), (shards_of,), jnp.float32, low / len(shards), high / len(shards))
        return jnp.repeat(jnp.exp(draws), dims[dim] // shards_of).reshape((-1,) + (1,) * (len(dims) - dim - 1))

    loudness = one(*shards[0])
    for cut in shards[1:]:
        loudness = loudness * one(*cut)
    return loudness


def bell_draw(key, dims, spread, most, shards=(), kind=jnp.bfloat16):
    result = jax.random.normal(key, dims, jnp.float32) * spread
    if len(shards) > 0:
        result = block_scale(key, dims, shards, -0.22, 0.18) * result
    return jnp.clip(result, min=-most, max=most).astype(kind)


def setup_inputs(seed: int = 0) -> dict:
    key_of = jax.random.split(jax.random.key(seed), 9)
    hidden_in = bell_draw(key_of[0], (ROWS, D), 1.0, 6.0, ((0, 256),))
    norm_gain = jnp.clip(1.0 + 0.1 * jax.random.normal(key_of[1], (D,), jnp.float32), 0.5, 1.5).astype(jnp.bfloat16)
    query_weight = bell_draw(key_of[2], (D, H * HD), D ** -0.5, 0.046875, ((0, 8), (1, 32)))
    probe = bell_draw(key_of[3], (D, H * HD), D ** -0.5, 0.046875, ((0, 8), (1, 32)))
    key_values = bell_draw(key_of[4], (ROWS, KVH * 2 * HD), 1.0, 6.0, ((0, 256),))
    readout = bell_draw(key_of[5], (ROWS, H * HD), (H * HD) ** -0.5, 0.0625, ((0, 8), (1, 32)))
    lengths = draw_lengths(jax.random.fold_in(key_of[8], 71), 0)
    ref_margin = bell_draw(key_of[7], (PAIRS,), 1.0, 6.0, ((0, 8),), jnp.float32)
    return {"hidden_in": hidden_in, "norm_gain": norm_gain, "query_weight": query_weight, "probe": probe, "key_values": key_values, "readout": readout, "lengths": lengths, "ref_margin": ref_margin}


pair_beta = 0.5
norm_epsilon = 1e-05

def sequence_logp(query, key_values, readout, lengths, heads):
    seqs = query.shape[0]
    seq_len = query.shape[1]
    kv_heads = key_values.shape[2] // (2 * HD)
    group = heads // kv_heads
    shaped = query.reshape(seqs, seq_len, kv_heads, group, HD)
    pairs_kv = key_values.astype(jnp.float32).reshape(seqs, seq_len, kv_heads, 2, HD)
    keys = pairs_kv[:, :, :, 0, :]
    values = pairs_kv[:, :, :, 1, :]
    scores = jnp.einsum('stkgd,sjkd->skgtj', shaped, keys) * (1.0 / jnp.sqrt(jnp.float32(HD)))
    position = jnp.arange(seq_len, dtype=jnp.int32)
    causal = position[None, :] <= position[:, None]
    valid = position[None, None, :] < lengths[:, None, None]
    allowed = (causal[None, :, :] & valid)[:, None, None, :, :]
    scores = jnp.where(allowed, scores, jnp.float32(-1e+30))
    top = lax.optimization_barrier(jnp.max(scores, axis=-1, keepdims=True))
    weights = jnp.exp(scores - lax.stop_gradient(top))
    probs = weights / lax.optimization_barrier(jnp.sum(weights, axis=-1, keepdims=True))
    attended = jnp.einsum('skgtj,sjkd->stkgd', probs, values)
    direction = readout.astype(jnp.float32).reshape(seqs, seq_len, kv_heads, group, HD)
    term = lax.optimization_barrier(jnp.sum(attended * direction, axis=(2, 3, 4)))
    live = position[None, :] < lengths[:, None]
    return lax.optimization_barrier(jnp.sum(jnp.where(live, term, jnp.float32(0.0)), axis=1))

def pair_loss(logp, ref_margin):
    margin = pair_beta * (logp[:, 0] - logp[:, 1] - ref_margin)
    return jnp.sum(jax.nn.softplus(-margin))

def reference(hidden_in, norm_gain, query_weight, probe, key_values, readout, lengths, ref_margin):
    wide = hidden_in.astype(jnp.float32)
    stats = lax.optimization_barrier(jnp.mean(wide * wide, axis=1, keepdims=True))
    normed = (wide * lax.rsqrt(stats + norm_epsilon) * norm_gain.astype(jnp.float32)).astype(jnp.bfloat16)
    query = jnp.dot(normed, query_weight, preferred_element_type=jnp.float32)
    tangent = jnp.dot(normed, probe, preferred_element_type=jnp.float32)
    seqs = PAIRS * 2

    def loss_of_query(values_q):
        logp = sequence_logp(values_q.reshape(seqs, SEQ_LEN, H * HD), key_values.reshape(seqs, SEQ_LEN, KVH * 2 * HD), readout.reshape(seqs, SEQ_LEN, H * HD), lengths.reshape(seqs), H)
        return pair_loss(logp.reshape(PAIRS, 2), ref_margin)
    unused, hess = jax.jvp(jax.grad(loss_of_query), (query,), (tangent,))
    hess_rows = hess.astype(jnp.bfloat16)
    group_rows = ROWS // N_DP

    def add_group(total, index):
        start = (index * group_rows).astype(jnp.int32)
        block_n = lax.dynamic_slice_in_dim(normed, start, group_rows, 0)
        block_h = lax.dynamic_slice_in_dim(hess_rows, start, group_rows, 0)
        partial_sum = lax.dot_general(block_n, block_h, (((0,), (0,)), ((), ())), preferred_element_type=jnp.float32)
        rounded = lax.optimization_barrier(partial_sum.astype(jnp.bfloat16))
        return (total + rounded.astype(jnp.float32), None)
    start_total = jnp.zeros((D, H * HD), jnp.float32)
    total, unused_stack = lax.scan(add_group, start_total, jnp.arange(N_DP, dtype=jnp.int32))
    return total
```

```python
import jax
import jax.numpy as jnp
from jax import lax
from jax.sharding import Mesh
from jax.sharding import PartitionSpec as P

HD = 64
KVH = 8
NY, NX, NZ, NL, NC = 4, 2, 8, 2, 2
DP = NY * NX
EARLY = 5

pair_beta = 0.5
norm_epsilon = 1e-05

bf16 = jnp.bfloat16
f32 = jnp.float32
CHUNKS = (0, 1, -1, 2, -2, 3, -3, 4)


def toward(axis, size, shift):
    pairs = [((i + shift) % size, i) for i in range(size)]
    return lambda value: lax.ppermute(value, axis, pairs)


core_swap = toward("core", NC, 1)
lo_swap = toward("x_lo", NL, 1)
hi_swap = toward("x_hi", NX, 1)


def dot(a, b):
    return jnp.dot(a, b, preferred_element_type=f32)


def reduce_dp(partial):
    narrow = partial.astype(bf16).reshape(NY, NX, *partial.shape[1:])
    total = narrow[0].astype(f32)
    arrived = [toward("y", NY, -dy)(narrow[dy]) for dy in range(1, NY)]
    for part in arrived:
        total = total + part.astype(f32)
    other = hi_swap(total[1].astype(bf16))
    return total[0] + other.astype(f32)


def gather_dp(rows):
    both = jnp.stack([rows, hi_swap(rows)])
    return jnp.concatenate([both] + [toward("y", NY, dy)(both) for dy in range(1, NY)])


def attention(query, tangent, keys, values, readout, lengths, position):
    scale = f32(HD**-0.5)
    seq_len = keys.shape[1]
    live = position < lengths[:, None]
    read = jnp.where(live[:, :, None, None], readout, bf16(0))
    column = jnp.arange(seq_len, dtype=jnp.int32)
    allowed = (column <= position[:, :, None]) & (column < lengths[:, None, None])
    allowed = allowed[:, :, None, :]
    scores = jnp.einsum("kthd,kjd->kthj", query, keys, preferred_element_type=f32) * scale
    slope = jnp.einsum("kthd,kjd->kthj", tangent, keys, preferred_element_type=f32) * scale
    gain = jnp.einsum("kthd,kjd->kthj", read, values, preferred_element_type=f32)
    scores = jnp.where(allowed, scores, f32(-1e30))
    weights = jnp.exp(scores - jnp.max(scores, axis=-1, keepdims=True))
    probs = weights / jnp.sum(weights, axis=-1, keepdims=True)
    mean_gain = jnp.sum(probs * gain, axis=-1, keepdims=True)
    mean_slope = jnp.sum(probs * slope, axis=-1, keepdims=True)
    lean = gain - mean_gain
    drift = slope - mean_slope
    mean_tan = jnp.sum(probs * lean * drift, axis=-1, keepdims=True)
    logp = jnp.sum(mean_gain, axis=(1, 2, 3))
    logp_tan = jnp.sum(mean_tan, axis=(1, 2, 3))
    return logp, logp_tan, (probs, lean, drift, mean_tan)


def shards(hidden_in, norm_gain, query_weight, probe, key_values, readout, lengths, ref_margin):
    iy, ix, iz, il, ic = (lax.axis_index(a) for a in ("y", "x_hi", "z", "x_lo", "core"))
    tensor = ("z", "x_lo", "core")
    rows_here, width = hidden_in.shape
    feats, columns = query_weight.shape

    both_q, both_t = (core_swap(query_weight), core_swap(probe))
    weights = jnp.concatenate([query_weight, both_q, probe, both_t], axis=1)

    wide = hidden_in.astype(f32)
    stats = jnp.mean(wide * wide, axis=1, keepdims=True)
    normed = (wide * lax.rsqrt(stats + norm_epsilon) * norm_gain.astype(f32)).astype(bf16)

    own = lax.all_to_all(normed, ("y", "x_hi"), split_axis=1, concat_axis=0, tiled=True)
    own = own.reshape(NY, NX, rows_here, feats)
    own = lax.dynamic_slice_in_dim(jnp.concatenate([own, own]), iy, NY, 0)
    own = jnp.where(ix == 0, own, own[:, ::-1]).reshape(DP, rows_here, feats)

    heads_kv = key_values.reshape(rows_here, KVH, 2 * HD).swapaxes(0, 1)
    heads_kv = jnp.broadcast_to(heads_kv[:, None], (KVH, NL * NC, rows_here, 2 * HD))
    kv = lax.all_to_all(
        heads_kv.reshape(NZ * NL * NC, rows_here, 2 * HD), tensor, split_axis=0, concat_axis=0, tiled=True
    )

    up, down = toward("z", NZ, -1), toward("z", NZ, 1)
    message = {0: jnp.concatenate([own, lo_swap(own[EARLY:])])}
    message[1], message[-1] = down(message[0]), up(message[0])
    message[2], message[-2] = down(message[1]), up(message[-1])
    message[3], message[-3] = down(message[2]), up(message[-2])
    half = message[0].shape[0] // 2
    message[4] = jnp.concatenate([down(message[3][:half]), up(message[-3][half:])])
    late = {k: lo_swap(message[k][:EARLY]) for k in CHUNKS}

    def chunk_rows(k):
        other = jnp.concatenate([late[k], message[k][DP:]])
        return jnp.stack([message[k][:DP], other], axis=1)

    groups = ((0, 1, -1), (2, -2), (3, -3), (4,))
    assert sum(groups, ()) == CHUNKS
    gathered, products = [], []
    for group in groups:
        block = jnp.stack([chunk_rows(k) for k in group], axis=1)
        gathered.append(block.reshape(DP, -1, feats))
        part = dot(block.reshape(-1, feats), weights)
        products.append(reduce_dp(part.reshape(DP, -1, 4 * columns)))
    normed_all = jnp.concatenate(gathered, axis=1)
    projected = jnp.concatenate(products)

    count = len(CHUNKS)
    tokens = NL * rows_here
    source = [lax.rem(iz + (k + NZ), NZ) for k in CHUNKS]
    seqs = lengths.shape[0] * 2
    per_seq = NZ // seqs
    seq_len = per_seq * NL * NC * rows_here
    sequence = jnp.stack([s // per_seq for s in source])
    flat_lengths = lengths.reshape(seqs)
    length = jnp.stack([lax.dynamic_index_in_dim(flat_lengths, s // per_seq, 0, False) for s in source])
    side = jnp.stack([il, 1 - il])
    place = jnp.stack([lax.rem(s, per_seq) for s in source])
    position = (
        ((place[:, None] * NL + side[None, :]) * NC + ic)[:, :, None] * rows_here
        + jnp.arange(rows_here, dtype=jnp.int32)
    ).reshape(count, tokens)
    kv = kv.reshape(seqs, seq_len, 2 * HD)
    kv = jnp.stack([lax.dynamic_index_in_dim(kv, s // per_seq, 0, False) for s in source])
    read = readout.reshape(NZ, NL, NC, rows_here, columns)
    mine = lax.dynamic_index_in_dim(read, ic, 2, False)
    theirs = lax.dynamic_index_in_dim(read, 1 - ic, 2, False)
    read = jnp.concatenate([mine, core_swap(theirs)], axis=-1)
    read = jnp.where(il == 0, read, read[:, ::-1])
    read = jnp.stack([lax.dynamic_index_in_dim(read, s, 0, False) for s in source])

    split = lambda v: v.reshape(count, tokens, -1, HD)
    query, tangent = (split(v.astype(bf16)) for v in jnp.split(projected, 2, axis=1))
    logp, logp_tan, (probs, lean, drift, mean_tan) = attention(
        query, tangent, kv[..., :HD], kv[..., HD:], split(read), length, position
    )

    here = sequence[:, None] == jnp.arange(seqs)
    sums = jnp.stack([jnp.sum(jnp.where(here, v[:, None], f32(0)), axis=0) for v in (logp, logp_tan)])
    spread = jnp.broadcast_to(sums[None], (NZ * NL * NC, 2, seqs))
    sums = jnp.sum(lax.all_to_all(spread, tensor, split_axis=0, concat_axis=0, tiled=True), axis=0)
    sums = sums.reshape(2, seqs // 2, 2)
    margin = pair_beta * (sums[0, :, 0] - sums[0, :, 1] - ref_margin)
    margin_tan = pair_beta * (sums[1, :, 0] - sums[1, :, 1])
    sure, unsure = jax.nn.sigmoid(margin), jax.nn.sigmoid(-margin)
    sign = jnp.array([-pair_beta, pair_beta], f32)
    coeff = (unsure[:, None] * sign).reshape(seqs)
    coeff_tan = (-(unsure * sure * margin_tan)[:, None] * sign).reshape(seqs)
    pick = lambda v: jnp.sum(jnp.where(here, v, f32(0)), axis=1)[:, None, None, None]
    coeff, coeff_tan = pick(coeff), pick(coeff_tan)
    bend = probs * (lean * (coeff_tan + coeff * drift) - coeff * mean_tan)
    hess = jnp.einsum("kthj,kjd->kthd", bend, kv[..., :HD], preferred_element_type=f32) * f32(HD**-0.5)
    hess_rows = hess.astype(bf16).reshape(count * tokens, 2 * columns)

    hess_all = gather_dp(hess_rows)
    left = normed_all.reshape(-1, feats)
    right = hess_all.reshape(-1, 2 * columns)
    outer = lambda b: lax.dot_general(left, b, (((0,), (0,)), ((), ())), preferred_element_type=f32)
    theirs = core_swap(outer(right[:, columns:]).astype(bf16))
    return outer(right[:, :columns]) + theirs.astype(f32)


def solution(mesh):
    fine = Mesh(
        mesh.devices.reshape(NY, NX, NZ, NL, NC), ("y", "x_hi", "z", "x_lo", "core")
    )
    dp, tensor = ("y", "x_hi"), ("z", "x_lo", "core")
    return jax.shard_map(
        shards,
        mesh=fine,
        in_specs=(
            P(dp + tensor, None),
            P(),
            P(dp, tensor),
            P(dp, tensor),
            P(dp + tensor, None),
            P(dp, tensor),
            P(dp, None),
            P(dp),
        ),
        out_specs=P(dp, tensor),
        check_vma=False,
    )
```

```python
import functools

import jax
import jax.numpy as jnp
from jax import lax
from jax.experimental import pallas as pl
from jax.experimental.pallas import tpu as pltpu
from jax.sharding import Mesh
from jax.sharding import PartitionSpec as P

HD = 64
KVH = 8
NY, NX, NZ, NL, NC = 4, 2, 8, 2, 2
DP = NY * NX
EARLY = 3

pair_beta = 0.5
norm_epsilon = 1e-05

bf16 = jnp.bfloat16
f32 = jnp.float32
CHUNKS = (0, 1, -1, 2, -2, 3, -3, 4)
LANES = 128


def toward(axis, size, shift):
    pairs = [((i + shift) % size, i) for i in range(size)]
    return lambda value: lax.ppermute(value, axis, pairs)


core_swap = toward("core", NC, 1)
lo_swap = toward("x_lo", NL, 1)
hi_swap = toward("x_hi", NX, 1)


def from_dp(dy, dx, dl, value):
    pairs = []
    for y in range(NY):
        for x in range(NX):
            for l in range(NL):
                source = (((y + dy) % NY) * NX + (x ^ dx)) * NL + (l ^ dl)
                pairs.append((source, (y * NX + x) * NL + l))
    return lax.ppermute(value, ("y", "x_hi", "x_lo"), pairs)


def together(*values):
    return lax.optimization_barrier(values)


def dot(a, b):
    return jnp.dot(a, b, preferred_element_type=f32)


def send_y(partial):
    split = partial.reshape(NY, NX, *partial.shape[1:])
    return [split[0]] + [toward("y", NY, -dy)(split[dy]) for dy in range(1, NY)]


def add_y(parts):
    total = parts[0].astype(f32)
    for part in parts[1:]:
        total = total + part.astype(f32)
    return total


def attention_kernel(chunks, heads, seq_ref, both_ref, read_ref, keys_ref, values_ref, limit_ref, grad_ref, tan_ref, sums_ref):
    rows = both_ref.shape[0] // chunks
    half = heads * HD
    scale = f32(HD**-0.5)
    nt = (((1,), (1,)), ((), ()))
    lane = lax.broadcasted_iota(jnp.int32, (rows, LANES), 1)
    out_lane = lax.broadcasted_iota(jnp.int32, (1, LANES), 1)
    sums = jnp.zeros((1, LANES), f32)
    for k in range(chunks):
        here = pl.ds(k * rows, rows)
        allowed = lane <= limit_ref[here, :]
        keys, values = keys_ref[k].astype(bf16), values_ref[k].astype(bf16)
        logp = jnp.zeros((rows, 1), f32)
        logp_tan = jnp.zeros((rows, 1), f32)
        for pair in range(heads // 2):
            cols = slice(pair * LANES, (pair + 1) * LANES)
            query = both_ref[here, cols].astype(bf16)
            tangent = both_ref[here, half + pair * LANES : half + (pair + 1) * LANES].astype(bf16)
            scores2 = lax.dot_general(query, keys, nt, preferred_element_type=f32) * scale
            slope2 = lax.dot_general(tangent, keys, nt, preferred_element_type=f32) * scale
            gain2 = lax.dot_general(read_ref[here, cols].astype(bf16), values, nt, preferred_element_type=f32)
            first, second = [], []
            for head in range(2):
                part = slice(head * LANES, (head + 1) * LANES)
                scores = jnp.where(allowed, scores2[:, part], f32(-1e30))
                slope, gain = slope2[:, part], gain2[:, part]
                weights = jnp.exp(scores - jnp.max(scores, axis=1, keepdims=True))
                probs = weights / jnp.sum(weights, axis=1, keepdims=True)
                mean_gain = jnp.sum(probs * gain, axis=1, keepdims=True)
                mean_slope = jnp.sum(probs * slope, axis=1, keepdims=True)
                lean = gain - mean_gain
                pull = probs * (slope - mean_slope)
                mean_tan = jnp.sum(pull * lean, axis=1, keepdims=True)
                first.append((probs * lean).astype(bf16))
                second.append((pull * lean - probs * mean_tan).astype(bf16))
                logp = logp + mean_gain
                logp_tan = logp_tan + mean_tan
            grad_ref[here, cols] = dot(jnp.concatenate(first, axis=1), keys) * scale
            tan_ref[here, cols] = dot(jnp.concatenate(second, axis=1), keys) * scale
        at = seq_ref[k]
        sums = sums + jnp.where(out_lane == at, jnp.sum(logp), f32(0))
        sums = sums + jnp.where(out_lane == at + LANES // 2, jnp.sum(logp_tan), f32(0))
    sums_ref[...] = sums


def attention(seq, both, read, keys, values, limit):
    chunks = keys.shape[0]
    rows, columns = read.shape
    vmem = pl.BlockSpec(memory_space=pltpu.VMEM)
    return pl.pallas_call(
        functools.partial(attention_kernel, chunks, columns // HD),
        out_shape=(
            jax.ShapeDtypeStruct((rows, columns), f32),
            jax.ShapeDtypeStruct((rows, columns), f32),
            jax.ShapeDtypeStruct((1, LANES), f32),
        ),
        in_specs=[pl.BlockSpec(memory_space=pltpu.SMEM)] + [vmem] * 5,
        out_specs=(vmem, vmem, vmem),
        compiler_params=pltpu.CompilerParams(vmem_limit_bytes=24 * 1024 * 1024),
    )(seq, both, read, keys, values, limit)


def combine_kernel(chunks, seqs, seq_ref, margin_ref, spread_ref, grad_ref, tan_ref, out_ref):
    total = jnp.sum(spread_ref[...], axis=0, keepdims=True)
    lane = lax.broadcasted_iota(jnp.int32, (1, LANES), 1)
    at = lambda i: jnp.sum(jnp.where(lane == i, total, f32(0)), axis=1, keepdims=True)
    coeffs = []
    for p in range(seqs // 2):
        margin = pair_beta * (at(2 * p) - at(2 * p + 1) - margin_ref[p])
        margin_tan = pair_beta * (at(LANES // 2 + 2 * p) - at(LANES // 2 + 2 * p + 1))
        sure, unsure = jax.nn.sigmoid(margin), jax.nn.sigmoid(-margin)
        slope = -pair_beta * unsure
        bend = pair_beta * unsure * sure * margin_tan
        coeffs += [(slope, bend), (-slope, -bend)]
    rows = grad_ref.shape[0] // chunks
    for k in range(chunks):
        coeff, coeff_tan = coeffs[0]
        for s in range(1, seqs):
            coeff = jnp.where(seq_ref[k] == s, coeffs[s][0], coeff)
            coeff_tan = jnp.where(seq_ref[k] == s, coeffs[s][1], coeff_tan)
        here = pl.ds(k * rows, rows)
        out_ref[here, :] = coeff_tan * grad_ref[here, :] + coeff * tan_ref[here, :]


def combine(seq, ref_margin, spread, grad, tan, seqs):
    chunks = seq.shape[0]
    vmem, smem = pl.BlockSpec(memory_space=pltpu.VMEM), pl.BlockSpec(memory_space=pltpu.SMEM)
    return pl.pallas_call(
        functools.partial(combine_kernel, chunks, seqs),
        out_shape=jax.ShapeDtypeStruct(grad.shape, f32),
        in_specs=[smem, smem, vmem, vmem, vmem],
        out_specs=vmem,
    )(seq, ref_margin, spread, grad, tan)


def shards(hidden_in, norm_gain, query_weight, probe, key_values, readout, lengths, ref_margin):
    iy, ix, iz, il, ic = (lax.axis_index(a) for a in ("y", "x_hi", "z", "x_lo", "core"))
    tensor = ("z", "x_lo", "core")
    rows_here, width = hidden_in.shape
    feats, columns = query_weight.shape

    wide = hidden_in.astype(f32)
    stats = jnp.mean(wide * wide, axis=1, keepdims=True)
    normed = (wide * lax.rsqrt(stats + norm_epsilon) * norm_gain.astype(f32)).astype(bf16)

    parts = normed.reshape(rows_here, NY, NX, feats).transpose(1, 2, 0, 3)
    parts = lax.dynamic_slice_in_dim(jnp.concatenate([parts, parts]), iy, NY, 0)
    parts = jnp.where(ix == 0, parts, parts[:, ::-1])
    (parts,) = together(parts)
    places = [(dy, dx) for dy in range(NY) for dx in range(NX)]
    block = lambda dy, dx: parts[(NY - dy) % NY, dx]
    own = [block(0, 0)] + [from_dp(dy, dx, 0, block(dy, dx)) for dy, dx in places[1:]]
    early = [from_dp(dy, dx, 1, block(dy, dx)) for dy, dx in places[:EARLY]]
    message = {0: jnp.stack(own + early)}

    other_q, other_t = core_swap(query_weight), core_swap(probe)
    (message[0], other_q, other_t) = together(message[0], other_q, other_t)
    weights = jnp.concatenate([query_weight, other_q, probe, other_t], axis=1)

    count = len(CHUNKS)
    tokens = NL * rows_here
    source = [lax.rem(iz + (k + NZ), NZ) for k in CHUNKS]
    seqs = lengths.shape[0] * 2
    per_seq = NZ // seqs
    seq_len = per_seq * NL * NC * rows_here
    sequence = jnp.stack([s // per_seq for s in source])
    flat_lengths = lengths.reshape(seqs)
    length = jnp.stack([lax.dynamic_index_in_dim(flat_lengths, s // per_seq, 0, False) for s in source])

    def prepare(token):
        heads_kv, theirs, ready = together(key_values, readout, token)
        heads_kv = heads_kv.reshape(rows_here, KVH, 2 * HD).swapaxes(0, 1)
        heads_kv = jnp.broadcast_to(heads_kv[:, None], (KVH, NL * NC, rows_here, 2 * HD))
        kv = lax.all_to_all(
            heads_kv.reshape(NZ * NL * NC, rows_here, 2 * HD), tensor, split_axis=0, concat_axis=0, tiled=True
        )
        kv = kv.reshape(seqs, seq_len, 2 * HD)
        kv = jnp.stack([lax.dynamic_index_in_dim(kv, s // per_seq, 0, False) for s in source])
        keys, values = kv[..., :HD].astype(f32), kv[..., HD:].astype(f32)
        empty = jnp.zeros_like(keys)
        diagonal = lambda v: jnp.concatenate(
            [jnp.concatenate([v, empty], axis=2), jnp.concatenate([empty, v], axis=2)], axis=1
        )
        side = jnp.stack([il, 1 - il])
        place = jnp.stack([lax.rem(s, per_seq) for s in source])
        position = (
            ((place[:, None] * NL + side[None, :]) * NC + ic)[:, :, None] * rows_here
            + jnp.arange(rows_here, dtype=jnp.int32)
        ).reshape(count, tokens)
        live = position < length[:, None]
        limit = jnp.minimum(position, length[:, None] - 1).reshape(count * tokens, 1)
        limit = jnp.broadcast_to(limit, (count * tokens, LANES))
        read = theirs.reshape(NZ, NL, NC, rows_here, columns)
        mine = lax.dynamic_index_in_dim(read, ic, 2, False)
        theirs = lax.dynamic_index_in_dim(read, 1 - ic, 2, False)
        read = jnp.concatenate([mine, core_swap(theirs)], axis=-1)
        read = jnp.where(il == 0, read, read[:, ::-1])
        read = jnp.stack([lax.dynamic_index_in_dim(read, s, 0, False) for s in source])
        read = read.reshape(count * tokens, 2 * columns)
        read = jnp.where(live.reshape(count * tokens, 1), read.astype(f32), f32(0))
        return read, diagonal(keys), diagonal(values), limit

    up, down = toward("z", NZ, -1), toward("z", NZ, 1)

    def rows_of(k, late):
        other = jnp.concatenate([message[k][DP:], late])
        return jnp.stack([message[k][:DP], other], axis=1)

    def multiply(group, late):
        block = jnp.stack([rows_of(k, late[k]) for k in group], axis=1).reshape(DP, -1, feats)
        part = dot(block.reshape(-1, feats), weights).astype(bf16)
        return block, part.reshape(DP, block.shape[1], 4 * columns)

    late = {}
    message[1], message[-1] = down(message[0]), up(message[0])
    late[0] = lo_swap(message[0][EARLY:DP])
    prepared = prepare(message[0])
    message[1], message[-1], late[0], *prepared = together(message[1], message[-1], late[0], *prepared)
    message[2], message[-2] = down(message[1]), up(message[-1])
    late[1], late[-1] = lo_swap(message[1][EARLY:DP]), lo_swap(message[-1][EARLY:DP])
    block_a, part_a = multiply((0,), late)
    message[2], message[-2], late[1], late[-1], block_a, part_a = together(
        message[2], message[-2], late[1], late[-1], block_a, part_a
    )
    message[3], message[-3] = down(message[2]), up(message[-2])
    late[2], late[-2] = lo_swap(message[2][EARLY:DP]), lo_swap(message[-2][EARLY:DP])
    block_b, part_b = multiply((1, -1), late)
    moved_a = send_y(part_a)
    message[3], message[-3], late[2], late[-2], block_b, part_b, *moved_a = together(
        message[3], message[-3], late[2], late[-2], block_b, part_b, *moved_a
    )
    half = message[0].shape[0] // 2
    ends = down(message[3][:half]), up(message[-3][half:])
    late[3], late[-3] = lo_swap(message[3][EARLY:DP]), lo_swap(message[-3][EARLY:DP])
    moved_b = send_y(part_b)
    block_c, part_c = multiply((2, -2), late)
    *ends, late[3], late[-3], block_c, part_c = together(*ends, late[3], late[-3], block_c, part_c)
    message[4] = jnp.concatenate(ends)
    late[4] = lo_swap(message[4][EARLY:DP])
    moved_c = send_y(part_c)
    block_d, part_d = multiply((3, -3), late)
    total_ab = jnp.concatenate([add_y(moved_a), add_y(moved_b)], axis=1)
    cross_ab = hi_swap(total_ab[1].astype(bf16))
    late[4], block_d, part_d, total_ab, cross_ab, *moved_c = together(
        late[4], block_d, part_d, total_ab, cross_ab, *moved_c
    )
    moved_d = send_y(part_d)
    block_e, part_e = multiply((4,), late)
    moved_e = send_y(part_e)
    total_c = add_y(moved_c)
    cross_c = hi_swap(total_c[1].astype(bf16))
    total_de = jnp.concatenate([add_y(moved_d), add_y(moved_e)], axis=1)
    cross_de = hi_swap(total_de[1].astype(bf16))
    own_sum = jnp.concatenate([total_ab[0], total_c[0], total_de[0]])
    projected = own_sum + jnp.concatenate([cross_ab, cross_c, cross_de]).astype(f32)
    normed_all = jnp.concatenate([block_a, block_b, block_c, block_d, block_e], axis=1)

    grad, tan, sums = attention(sequence, projected, *prepared)
    spread = jnp.broadcast_to(sums[None], (NZ * NL * NC, 1, LANES))
    spread = lax.all_to_all(spread, tensor, split_axis=0, concat_axis=0, tiled=True).reshape(-1, LANES)
    hess_rows = combine(sequence, ref_margin, spread, grad, tan, seqs).astype(bf16)

    y_gather = lambda v: jnp.stack([v] + [toward("y", NY, dy)(v) for dy in range(1, NY)])
    hess_own, hess_other = hess_rows[:, :columns], hess_rows[:, columns:]
    other_all = y_gather(jnp.stack([hess_other, hi_swap(hess_other)]))
    own_y = y_gather(hess_own)
    own_all = jnp.stack([own_y, hi_swap(own_y)], axis=1)
    left = normed_all.reshape(-1, feats)
    outer = lambda b: lax.dot_general(
        left, b.reshape(-1, columns), (((0,), (0,)), ((), ())), preferred_element_type=f32
    )
    theirs = core_swap(outer(other_all).astype(bf16))
    return outer(own_all) + theirs.astype(f32)


def solution(mesh):
    fine = Mesh(
        mesh.devices.reshape(NY, NX, NZ, NL, NC), ("y", "x_hi", "z", "x_lo", "core")
    )
    dp, tensor = ("y", "x_hi"), ("z", "x_lo", "core")
    return jax.shard_map(
        shards,
        mesh=fine,
        in_specs=(
            P(dp + tensor, None),
            P(),
            P(dp, tensor),
            P(dp, tensor),
            P(dp + tensor, None),
            P(dp, tensor),
            P(dp, None),
            P(dp),
        ),
        out_specs=P(dp, tensor),
        check_vma=False,
    )
```

```python
import functools

import jax
import jax.numpy as jnp
from jax import lax
from jax.experimental import pallas as pl
from jax.experimental.pallas import tpu as pltpu
from jax.sharding import Mesh
from jax.sharding import PartitionSpec as P

HD = 64
KVH = 8
NY, NX, NZ, NL, NC = 4, 2, 8, 2, 2
DP = NY * NX
EARLY = 3

pair_beta = 0.5
norm_epsilon = 1e-05

bf16 = jnp.bfloat16
f32 = jnp.float32
CHUNKS = (0, 1, -1, 2, -2, 3, -3, 4)
LANES = 128


def toward(axis, size, shift):
    pairs = [((i + shift) % size, i) for i in range(size)]
    return lambda value: lax.ppermute(value, axis, pairs)


core_swap = toward("core", NC, 1)
lo_swap = toward("x_lo", NL, 1)
hi_swap = toward("x_hi", NX, 1)


def together(*values):
    return lax.optimization_barrier(values)


def dot(a, b):
    return jnp.dot(a, b, preferred_element_type=f32)


def reduce_y(partial, iy):
    split = partial.reshape(NY, NX, *partial.shape[1:])
    block = lambda dy: lax.dynamic_index_in_dim(split, lax.rem(iy + dy, NY), 0, False)
    total = block(0).astype(f32)
    for part in [toward("y", NY, -dy)(block(dy)) for dy in (2, 1, 3)]:
        total = total + part.astype(f32)
    return total


def hi_halves(total, ix):
    keep = lax.dynamic_index_in_dim(total, ix, 0, False)
    give = lax.dynamic_index_in_dim(total, 1 - ix, 0, False)
    return keep.astype(f32), hi_swap(give.astype(bf16))


def attention_kernel(info_ref, both_ref, read_ref, kv_ref, grad_ref, tan_ref, sums_ref, keys_ref, values_ref):
    places, sides, part_rows, columns = read_ref.shape
    seqs = kv_ref.shape[0]
    rows = sides * part_rows
    chunks = both_ref.shape[0] // rows
    pairs = columns // LANES
    per_seq = places // seqs
    scale = f32(HD**-0.5)
    nt = (((1,), (1,)), ((), ()))
    low = lax.broadcasted_iota(jnp.int32, (kv_ref.shape[1], LANES), 1) < HD
    for s in range(seqs):
        kv = kv_ref[s]
        turned = pltpu.roll(kv, HD, 1)
        keys_ref[s] = jnp.concatenate([jnp.where(low, kv, 0.0), jnp.where(low, 0.0, turned)]).astype(bf16)
        values_ref[s] = jnp.concatenate([jnp.where(low, turned, 0.0), jnp.where(low, 0.0, kv)]).astype(bf16)
    lane = lax.broadcasted_iota(jnp.int32, (part_rows, LANES), 1)
    row = lax.broadcasted_iota(jnp.int32, (part_rows, LANES), 0)
    out_lane = lax.broadcasted_iota(jnp.int32, (1, LANES), 1)
    x_lo, core = info_ref[chunks + seqs], info_ref[chunks + seqs + 1]
    stack = lambda blocks: jnp.concatenate(blocks, axis=0)
    column = lambda pair: slice(pair * LANES, (pair + 1) * LANES)
    sums = jnp.zeros((1, LANES), f32)
    for k in range(chunks):
        here = pl.ds(k * rows, rows)
        place = info_ref[k]
        seq = place // per_seq
        length = info_ref[chunks + seq]
        keys, values = keys_ref[seq], values_ref[seq]
        allowed, read = [], []
        for side in (x_lo, 1 - x_lo):
            position = ((place % per_seq * sides + side) * NC + core) * part_rows + row
            allowed.append(lane <= jnp.minimum(position, length - 1))
            live = position[:, :1] < length
            read.append(jnp.where(live, read_ref[place, side], 0.0))
        read = stack(read).astype(bf16)
        allowed = stack(allowed * pairs)
        both = both_ref[here, :].astype(bf16)
        both = lax.dot_general(
            stack([both[:, column(p)] for p in range(2 * pairs)]), keys, nt, preferred_element_type=f32
        )
        gain2 = lax.dot_general(
            stack([read[:, column(p)] for p in range(pairs)]), values, nt, preferred_element_type=f32
        )
        scores2, slope2 = both[: pairs * rows] * scale, both[pairs * rows :] * scale
        first, second = [], []
        logp = jnp.zeros((pairs * rows, 1), f32)
        logp_tan = jnp.zeros((pairs * rows, 1), f32)
        for head in range(2):
            part = column(head)
            scores = jnp.where(allowed, scores2[:, part], f32(-1e30))
            slope, gain = slope2[:, part], gain2[:, part]
            weights = jnp.exp(scores - jnp.max(scores, axis=1, keepdims=True))
            probs = weights / jnp.sum(weights, axis=1, keepdims=True)
            mean_gain = jnp.sum(probs * gain, axis=1, keepdims=True)
            mean_slope = jnp.sum(probs * slope, axis=1, keepdims=True)
            lean = gain - mean_gain
            pull = probs * (slope - mean_slope)
            mean_tan = jnp.sum(pull * lean, axis=1, keepdims=True)
            first.append((probs * lean).astype(bf16))
            second.append((pull * lean - probs * mean_tan).astype(bf16))
            logp = logp + mean_gain
            logp_tan = logp_tan + mean_tan
        out = dot(stack([jnp.concatenate(first, axis=1), jnp.concatenate(second, axis=1)]), keys) * scale
        for p in range(pairs):
            grad_ref[here, column(p)] = out[p * rows : (p + 1) * rows]
            tan_ref[here, column(p)] = out[(pairs + p) * rows : (pairs + p + 1) * rows]
        sums = sums + jnp.where(out_lane == seq, jnp.sum(logp), f32(0))
        sums = sums + jnp.where(out_lane == seq + LANES // 2, jnp.sum(logp_tan), f32(0))
    sums_ref[...] = sums


def attention(info, both, read, kv):
    rows, columns = both.shape[0], read.shape[-1]
    vmem = pl.BlockSpec(memory_space=pltpu.VMEM)
    return pl.pallas_call(
        attention_kernel,
        out_shape=(
            jax.ShapeDtypeStruct((rows, columns), f32),
            jax.ShapeDtypeStruct((rows, columns), f32),
            jax.ShapeDtypeStruct((1, LANES), f32),
        ),
        in_specs=[pl.BlockSpec(memory_space=pltpu.SMEM)] + [vmem] * 3,
        out_specs=(vmem, vmem, vmem),
        scratch_shapes=[pltpu.VMEM((kv.shape[0], 2 * kv.shape[1], LANES), bf16)] * 2,
        compiler_params=pltpu.CompilerParams(vmem_limit_bytes=24 * 1024 * 1024),
    )(info, both, read, kv)


def combine_kernel(chunks, seqs, info_ref, margin_ref, spread_ref, grad_ref, tan_ref, out_ref):
    total = jnp.sum(spread_ref[...], axis=0, keepdims=True)
    lane = lax.broadcasted_iota(jnp.int32, (1, LANES), 1)
    at = lambda i: jnp.sum(jnp.where(lane == i, total, f32(0)), axis=1, keepdims=True)
    coeffs = []
    for p in range(seqs // 2):
        margin = pair_beta * (at(2 * p) - at(2 * p + 1) - margin_ref[p])
        margin_tan = pair_beta * (at(LANES // 2 + 2 * p) - at(LANES // 2 + 2 * p + 1))
        sure, unsure = jax.nn.sigmoid(margin), jax.nn.sigmoid(-margin)
        slope = -pair_beta * unsure
        bend = pair_beta * unsure * sure * margin_tan
        coeffs += [(slope, bend), (-slope, -bend)]
    rows = grad_ref.shape[0] // chunks
    per_seq = NZ // seqs
    for k in range(chunks):
        seq = info_ref[k] // per_seq
        coeff, coeff_tan = coeffs[0]
        for s in range(1, seqs):
            coeff = jnp.where(seq == s, coeffs[s][0], coeff)
            coeff_tan = jnp.where(seq == s, coeffs[s][1], coeff_tan)
        here = pl.ds(k * rows, rows)
        out_ref[here, :] = coeff_tan * grad_ref[here, :] + coeff * tan_ref[here, :]


def combine(info, ref_margin, spread, grad, tan, seqs):
    vmem, smem = pl.BlockSpec(memory_space=pltpu.VMEM), pl.BlockSpec(memory_space=pltpu.SMEM)
    return pl.pallas_call(
        functools.partial(combine_kernel, len(CHUNKS), seqs),
        out_shape=jax.ShapeDtypeStruct(grad.shape, f32),
        in_specs=[smem, smem, vmem, vmem, vmem],
        out_specs=vmem,
    )(info, ref_margin, spread, grad, tan)


def shards(hidden_in, norm_gain, query_weight, probe, key_values, readout, lengths, ref_margin):
    iy, ix, iz, il, ic = (lax.axis_index(a) for a in ("y", "x_hi", "z", "x_lo", "core"))
    tensor = ("z", "x_lo", "core")
    rows_here, width = hidden_in.shape
    feats, columns = query_weight.shape

    wide = hidden_in.astype(f32)
    stats = jnp.mean(wide * wide, axis=1, keepdims=True)
    normed = (wide * lax.rsqrt(stats + norm_epsilon) * norm_gain.astype(f32)).astype(bf16)

    own = lax.all_to_all(normed, ("y", "x_hi"), split_axis=1, concat_axis=0, tiled=True)
    own = own.reshape(DP, rows_here, feats)
    other_q, other_t = core_swap(query_weight), core_swap(probe)
    own, other_q, other_t = together(own, other_q, other_t)
    message = {0: jnp.concatenate([own, lo_swap(own[:EARLY])])}
    (message[0],) = together(message[0])

    seqs = lengths.shape[0] * 2
    seq_len = NZ // seqs * NL * NC * rows_here

    def prepare(token):
        heads_kv, read, first, second, third, fourth, length, _ = together(
            key_values, readout, query_weight, other_q, probe, other_t, lengths, token
        )
        weights = jnp.concatenate([first, second, third, fourth], axis=1)
        heads_kv = heads_kv.reshape(rows_here, KVH, 2 * HD).swapaxes(0, 1)
        heads_kv = jnp.broadcast_to(heads_kv[:, None], (KVH, NL * NC, rows_here, 2 * HD))
        kv = lax.all_to_all(
            heads_kv.reshape(NZ * NL * NC, rows_here, 2 * HD), tensor, split_axis=0, concat_axis=0, tiled=True
        )
        kv = kv.reshape(seqs, seq_len, 2 * HD).astype(f32)
        read = read.reshape(NZ, NL, NC, rows_here, columns)
        mine = lax.dynamic_index_in_dim(read, ic, 2, False)
        theirs = lax.dynamic_index_in_dim(read, 1 - ic, 2, False)
        read = jnp.concatenate([mine, core_swap(theirs)], axis=-1).astype(f32)
        info = jnp.concatenate(
            [(iz + jnp.array(CHUNKS, jnp.int32) + NZ) % NZ, length.reshape(seqs), jnp.stack([il, ic])]
        )
        return weights, info, read, kv

    up, down = toward("z", NZ, -1), toward("z", NZ, 1)

    def rows_of(k):
        return jnp.stack([message[k][:DP], jnp.concatenate([message[k][DP:], late[k]])], axis=1)

    def multiply(group):
        block = jnp.stack([rows_of(k) for k in group], axis=1).reshape(DP, -1, feats)
        part = dot(block.reshape(-1, feats), weights).astype(bf16)
        return block, part.reshape(DP, block.shape[1], 4 * columns)

    def swap_late(k):
        both = lo_swap(jnp.stack([message[k][EARLY:DP], message[-k][EARLY:DP]]))
        return both[0], both[1]

    late = {}
    message[1], message[-1] = down(message[0]), up(message[0])
    late[0] = lo_swap(own[EARLY:])
    prepared = prepare(message[0])
    message[1], message[-1], late[0], *prepared = together(message[1], message[-1], late[0], *prepared)
    weights, info, read, kv = prepared
    message[2], message[-2] = down(message[1]), up(message[-1])
    late[1], late[-1] = swap_late(1)
    message[2], message[-2], late[1], late[-1] = together(message[2], message[-2], late[1], late[-1])
    message[3], message[-3] = down(message[2]), up(message[-2])
    late[2], late[-2] = swap_late(2)
    block_a, part_a = multiply((0, 1, -1))
    total_a = lax.psum_scatter(part_a.reshape(NY, -1, 4 * columns), "y", scatter_dimension=0, tiled=True)
    message[3], message[-3], late[2], late[-2], block_a = together(
        message[3], message[-3], late[2], late[-2], block_a
    )
    half = message[0].shape[0] // 2
    ends = down(message[3][:half]), up(message[-3][half:])
    late[3], late[-3] = swap_late(3)
    block_b, part_b = multiply((2, -2))
    total_b = reduce_y(part_b, iy)
    *ends, late[3], late[-3], block_b = together(*ends, late[3], late[-3], block_b)
    message[4] = jnp.concatenate(ends)
    late[4] = lo_swap(message[4][EARLY:DP])
    total_a = total_a.reshape(NX, -1, 4 * columns)
    keep_a, cross_a = hi_halves(total_a, ix)
    late[4], keep_a, total_b = together(late[4], keep_a, total_b)
    block_c, part_c = multiply((3, -3, 4))
    keep_b, cross_b = hi_halves(total_b, ix)
    arrived = lax.all_to_all(part_c, ("y", "x_hi"), split_axis=0, concat_axis=0, tiled=True)
    total_c = jnp.sum(arrived.astype(f32), axis=0)
    projected = jnp.concatenate([keep_a + cross_a.astype(f32), keep_b + cross_b.astype(f32), total_c])
    normed_all = jnp.concatenate([block_a, block_b, block_c], axis=1)

    grad, tan, sums = attention(info, projected, read, kv)
    spread = jnp.broadcast_to(sums[None], (NZ * NL * NC, 1, LANES))
    spread = lax.all_to_all(spread, tensor, split_axis=0, concat_axis=0, tiled=True).reshape(-1, LANES)
    hess_rows = combine(info, ref_margin, spread, grad, tan, seqs).astype(bf16)

    hess_all = jnp.broadcast_to(hess_rows[None], (DP, *hess_rows.shape))
    hess_all = lax.all_to_all(hess_all, ("y", "x_hi"), split_axis=0, concat_axis=0, tiled=True)
    hess_all = hess_all.reshape(-1, 2 * columns)
    left = normed_all.reshape(-1, feats)
    outer = lambda b: lax.dot_general(left, b, (((0,), (0,)), ((), ())), preferred_element_type=f32)
    theirs = core_swap(outer(hess_all[:, columns:]).astype(bf16))
    return outer(hess_all[:, :columns]) + theirs.astype(f32)


def solution(mesh):
    fine = Mesh(
        mesh.devices.reshape(NY, NX, NZ, NL, NC), ("y", "x_hi", "z", "x_lo", "core")
    )
    dp, tensor = ("y", "x_hi"), ("z", "x_lo", "core")
    return jax.shard_map(
        shards,
        mesh=fine,
        in_specs=(
            P(dp + tensor, None),
            P(),
            P(dp, tensor),
            P(dp, tensor),
            P(dp + tensor, None),
            P(dp, tensor),
            P(dp, None),
            P(dp),
        ),
        out_specs=P(dp, tensor),
        check_vma=False,
    )
```

```python
import functools

import jax
import jax.numpy as jnp
from jax import lax
from jax.experimental import pallas as pl
from jax.experimental.pallas import tpu as pltpu
from jax.sharding import Mesh
from jax.sharding import PartitionSpec as P

HD = 64
KVH = 8
NY, NX, NZ, NL, NC = 4, 2, 8, 2, 2
DP = NY * NX

pair_beta = 0.5
norm_epsilon = 1e-05

bf16 = jnp.bfloat16
f32 = jnp.float32
CHUNKS = (0, 1, -1, 2, -2, 3, -3, 4)
LANES = 128


def toward(axis, size, shift):
    pairs = [((i + shift) % size, i) for i in range(size)]
    return lambda value: lax.ppermute(value, axis, pairs)


core_swap = toward("core", NC, 1)
hi_swap = toward("x_hi", NX, 1)


def together(*values):
    return lax.optimization_barrier(values)


def dot(a, b):
    return jnp.dot(a, b, preferred_element_type=f32)


def reduce_y(partial, iy):
    split = partial.reshape(partial.shape[0], NY, NX, *partial.shape[2:])
    block = lambda dy: lax.dynamic_index_in_dim(split, lax.rem(iy + dy, NY), 1, False)
    return [block(0)] + [toward("y", NY, -dy)(block(dy)) for dy in (2, 1, 3)]


def add(parts):
    total = parts[0].astype(f32)
    for part in parts[1:]:
        total = total + part.astype(f32)
    return total


def attention_kernel(info_ref, both_ref, read_ref, kv_ref, grad_ref, tan_ref, sums_ref, keys_ref, values_ref):
    places, sides, part_rows, columns = read_ref.shape
    seqs = kv_ref.shape[0]
    rows = sides * part_rows
    chunks = both_ref.shape[0] // rows
    pairs = columns // LANES
    per_seq = places // seqs
    scale = f32(HD**-0.5)
    nt = (((1,), (1,)), ((), ()))
    low = lax.broadcasted_iota(jnp.int32, (kv_ref.shape[1], LANES), 1) < HD
    for s in range(seqs):
        kv = kv_ref[s]
        turned = pltpu.roll(kv, HD, 1)
        keys_ref[s] = jnp.concatenate([jnp.where(low, kv, 0.0), jnp.where(low, 0.0, turned)]).astype(bf16)
        values_ref[s] = jnp.concatenate([jnp.where(low, turned, 0.0), jnp.where(low, 0.0, kv)]).astype(bf16)
    lane = lax.broadcasted_iota(jnp.int32, (part_rows, LANES), 1)
    row = lax.broadcasted_iota(jnp.int32, (part_rows, LANES), 0)
    out_lane = lax.broadcasted_iota(jnp.int32, (1, LANES), 1)
    core = info_ref[chunks + seqs]
    stack = lambda blocks: jnp.concatenate(blocks, axis=0)
    column = lambda pair: slice(pair * LANES, (pair + 1) * LANES)
    sums = jnp.zeros((1, LANES), f32)
    for k in range(chunks):
        here = pl.ds(k * rows, rows)
        place = info_ref[k]
        seq = place // per_seq
        length = info_ref[chunks + seq]
        keys, values = keys_ref[seq], values_ref[seq]
        allowed, read = [], []
        for side in range(sides):
            position = ((place % per_seq * sides + side) * NC + core) * part_rows + row
            allowed.append(lane <= jnp.minimum(position, length - 1))
            live = position[:, :1] < length
            read.append(jnp.where(live, read_ref[place, side], 0.0))
        read = stack(read).astype(bf16)
        allowed = stack(allowed * pairs)
        both = both_ref[here, :].astype(bf16)
        both = lax.dot_general(
            stack([both[:, column(p)] for p in range(2 * pairs)]), keys, nt, preferred_element_type=f32
        )
        gain2 = lax.dot_general(
            stack([read[:, column(p)] for p in range(pairs)]), values, nt, preferred_element_type=f32
        )
        scores2, slope2 = both[: pairs * rows] * scale, both[pairs * rows :] * scale
        first, second = [], []
        logp = jnp.zeros((pairs * rows, 1), f32)
        logp_tan = jnp.zeros((pairs * rows, 1), f32)
        for head in range(2):
            part = column(head)
            scores = jnp.where(allowed, scores2[:, part], f32(-1e30))
            slope, gain = slope2[:, part], gain2[:, part]
            weights = jnp.exp(scores - jnp.max(scores, axis=1, keepdims=True))
            probs = weights / jnp.sum(weights, axis=1, keepdims=True)
            mean_gain = jnp.sum(probs * gain, axis=1, keepdims=True)
            mean_slope = jnp.sum(probs * slope, axis=1, keepdims=True)
            lean = gain - mean_gain
            pull = probs * (slope - mean_slope)
            mean_tan = jnp.sum(pull * lean, axis=1, keepdims=True)
            first.append((probs * lean).astype(bf16))
            second.append((pull * lean - probs * mean_tan).astype(bf16))
            logp = logp + mean_gain
            logp_tan = logp_tan + mean_tan
        out = dot(stack([jnp.concatenate(first, axis=1), jnp.concatenate(second, axis=1)]), keys) * scale
        for p in range(pairs):
            grad_ref[here, column(p)] = out[p * rows : (p + 1) * rows]
            tan_ref[here, column(p)] = out[(pairs + p) * rows : (pairs + p + 1) * rows]
        sums = sums + jnp.where(out_lane == seq, jnp.sum(logp), f32(0))
        sums = sums + jnp.where(out_lane == seq + LANES // 2, jnp.sum(logp_tan), f32(0))
    sums_ref[...] = sums


def attention(info, both, read, kv):
    rows, columns = both.shape[0], read.shape[-1]
    vmem = pl.BlockSpec(memory_space=pltpu.VMEM)
    return pl.pallas_call(
        attention_kernel,
        out_shape=(
            jax.ShapeDtypeStruct((rows, columns), f32),
            jax.ShapeDtypeStruct((rows, columns), f32),
            jax.ShapeDtypeStruct((1, LANES), f32),
        ),
        in_specs=[pl.BlockSpec(memory_space=pltpu.SMEM)] + [vmem] * 3,
        out_specs=(vmem, vmem, vmem),
        scratch_shapes=[pltpu.VMEM((kv.shape[0], 2 * kv.shape[1], LANES), bf16)] * 2,
        compiler_params=pltpu.CompilerParams(vmem_limit_bytes=12 * 1024 * 1024),
    )(info, both, read, kv)


def combine_kernel(chunks, seqs, info_ref, margin_ref, spread_ref, grad_ref, tan_ref, out_ref):
    total = jnp.sum(spread_ref[...], axis=0, keepdims=True)
    lane = lax.broadcasted_iota(jnp.int32, (1, LANES), 1)
    at = lambda i: jnp.sum(jnp.where(lane == i, total, f32(0)), axis=1, keepdims=True)
    coeffs = []
    for p in range(seqs // 2):
        margin = pair_beta * (at(2 * p) - at(2 * p + 1) - margin_ref[p])
        margin_tan = pair_beta * (at(LANES // 2 + 2 * p) - at(LANES // 2 + 2 * p + 1))
        sure, unsure = jax.nn.sigmoid(margin), jax.nn.sigmoid(-margin)
        slope = -pair_beta * unsure
        bend = pair_beta * unsure * sure * margin_tan
        coeffs += [(slope, bend), (-slope, -bend)]
    rows = grad_ref.shape[0] // chunks
    per_seq = NZ // seqs
    for k in range(chunks):
        seq = info_ref[k] // per_seq
        coeff, coeff_tan = coeffs[0]
        for s in range(1, seqs):
            coeff = jnp.where(seq == s, coeffs[s][0], coeff)
            coeff_tan = jnp.where(seq == s, coeffs[s][1], coeff_tan)
        here = pl.ds(k * rows, rows)
        out_ref[here, :] = coeff_tan * grad_ref[here, :] + coeff * tan_ref[here, :]


def combine(info, ref_margin, spread, grad, tan, seqs):
    vmem, smem = pl.BlockSpec(memory_space=pltpu.VMEM), pl.BlockSpec(memory_space=pltpu.SMEM)
    return pl.pallas_call(
        functools.partial(combine_kernel, len(CHUNKS), seqs),
        out_shape=jax.ShapeDtypeStruct(grad.shape, f32),
        in_specs=[smem, smem, vmem, vmem, vmem],
        out_specs=vmem,
        compiler_params=pltpu.CompilerParams(vmem_limit_bytes=6 * 1024 * 1024),
    )(info, ref_margin, spread, grad, tan)


def shards(hidden_in, norm_gain, query_weight, probe, key_values, readout, lengths, ref_margin):
    iy, ix, iz, ic = (lax.axis_index(a) for a in ("y", "x_hi", "z", "core"))
    tensor = ("z", "x_lo", "core")
    rows_here, width = hidden_in.shape
    feats, columns = query_weight.shape

    wide = hidden_in.astype(f32)
    stats = jnp.mean(wide * wide, axis=1, keepdims=True)
    normed = (wide * lax.rsqrt(stats + norm_epsilon) * norm_gain.astype(f32)).astype(bf16)

    other_q, other_t = core_swap(query_weight), core_swap(probe)
    sides = normed.reshape(rows_here, DP, feats).swapaxes(0, 1)
    sides = jnp.broadcast_to(sides[:, None], (DP, NL, rows_here, feats))
    first = lax.all_to_all(
        sides.reshape(DP * NL, rows_here, feats), ("y", "x_hi", "x_lo"), split_axis=0, concat_axis=0, tiled=True
    )
    chunk = {}
    chunk[0], other_q, other_t = together(first, other_q, other_t)

    seqs = lengths.shape[0] * 2
    seq_len = NZ // seqs * NL * NC * rows_here
    up, down = toward("z", NZ, -1), toward("z", NZ, 1)

    def multiply(group):
        rows = jnp.concatenate([chunk[k] for k in group]).reshape(-1, feats)
        return dot(rows, weights).astype(bf16).reshape(len(group), DP, NL * rows_here, 4 * columns)

    chunk[1], chunk[-1] = down(chunk[0]), up(chunk[0])
    heads_kv, _ = together(key_values, chunk[0])
    heads_kv = heads_kv.reshape(rows_here, KVH, 2 * HD).swapaxes(0, 1)
    heads_kv = jnp.broadcast_to(heads_kv[:, None], (KVH, NL * NC, rows_here, 2 * HD))
    kv = lax.all_to_all(
        heads_kv.reshape(NZ * NL * NC, rows_here, 2 * HD), tensor, split_axis=0, concat_axis=0, tiled=True
    )
    weights = jnp.concatenate([query_weight, other_q, probe, other_t], axis=1)
    chunk[1], chunk[-1], kv, weights = together(chunk[1], chunk[-1], kv, weights)
    chunk[2], chunk[-2] = down(chunk[1]), up(chunk[-1])
    moved_a = reduce_y(multiply((0, 1, -1)), iy)
    chunk[2], chunk[-2], *moved_a = together(chunk[2], chunk[-2], *moved_a)
    chunk[3], chunk[-3] = down(chunk[2]), up(chunk[-2])
    moved_b = reduce_y(multiply((2, -2)), iy)
    total_a = add(moved_a)
    kv = kv.reshape(seqs, seq_len, 2 * HD).astype(f32)
    chunk[3], chunk[-3], total_a, kv, *moved_b = together(chunk[3], chunk[-3], total_a, kv, *moved_b)
    half = DP * NL // 2
    ends = down(chunk[3][:half]), up(chunk[-3][half:])
    moved_c = reduce_y(multiply((3, -3)), iy)
    total_b = add(moved_b)
    *ends, total_a, total_b = together(*ends, total_a, total_b)
    chunk[4] = jnp.concatenate(ends)
    read = readout.reshape(NZ, NL, NC, rows_here, columns)
    mine = lax.dynamic_index_in_dim(read, ic, 2, False)
    theirs = lax.dynamic_index_in_dim(read, 1 - ic, 2, False)
    read = jnp.concatenate([mine, core_swap(theirs)], axis=-1).astype(f32)
    info = jnp.concatenate([(iz + jnp.array(CHUNKS, jnp.int32) + NZ) % NZ, lengths.reshape(seqs), ic[None]])
    part_d = multiply((4,))[0]
    total = jnp.concatenate([total_a, total_b, add(moved_c)])
    keep = lax.dynamic_index_in_dim(total, ix, 1, False)
    cross = hi_swap(lax.dynamic_index_in_dim(total, 1 - ix, 1, False).astype(bf16))
    arrived = lax.all_to_all(part_d, ("y", "x_hi"), split_axis=0, concat_axis=0, tiled=True)
    last = jnp.sum(arrived.astype(f32), axis=0)
    projected = jnp.concatenate([(keep + cross.astype(f32)).reshape(-1, 4 * columns), last])
    normed_all = jnp.stack([chunk[k].reshape(DP, -1, feats) for k in CHUNKS], axis=1)

    grad, tan, sums = attention(info, projected, read, kv)
    spread = jnp.broadcast_to(sums[None], (NZ * NL * NC, 1, LANES))
    spread = lax.all_to_all(spread, tensor, split_axis=0, concat_axis=0, tiled=True).reshape(-1, LANES)
    hess_rows = combine(info, ref_margin, spread, grad, tan, seqs).astype(bf16)

    hess_all = jnp.broadcast_to(hess_rows[None], (DP, *hess_rows.shape))
    hess_all = lax.all_to_all(hess_all, ("y", "x_hi"), split_axis=0, concat_axis=0, tiled=True)
    hess_all = hess_all.reshape(-1, 2 * columns)
    left = normed_all.reshape(-1, feats)
    outer = lambda b: lax.dot_general(left, b, (((0,), (0,)), ((), ())), preferred_element_type=f32)
    theirs = core_swap(outer(hess_all[:, columns:]).astype(bf16))
    return outer(hess_all[:, :columns]) + theirs.astype(f32)


def solution(mesh):
    fine = Mesh(
        mesh.devices.reshape(NY, NX, NZ, NL, NC), ("y", "x_hi", "z", "x_lo", "core")
    )
    dp, tensor = ("y", "x_hi"), ("z", "x_lo", "core")
    return jax.shard_map(
        shards,
        mesh=fine,
        in_specs=(
            P(dp + tensor, None),
            P(),
            P(dp, tensor),
            P(dp, tensor),
            P(dp + tensor, None),
            P(dp, tensor),
            P(dp, None),
            P(dp),
        ),
        out_specs=P(dp, tensor),
        check_vma=False,
    )
```

```python
import functools

import jax
import jax.numpy as jnp
from jax import lax
from jax.experimental import pallas as pl
from jax.experimental.pallas import tpu as pltpu
from jax.sharding import Mesh
from jax.sharding import PartitionSpec as P

HD = 64
KVH = 8
NY, NX, NZ, NL, NC = 4, 2, 8, 2, 2
DP = NY * NX

pair_beta = 0.5
norm_epsilon = 1e-05

bf16 = jnp.bfloat16
f32 = jnp.float32
CHUNKS = (0, 1, -1, 2, -2, 3, -3, 4)
LANES = 128


def toward(axis, size, shift):
    pairs = [((i + shift) % size, i) for i in range(size)]
    return lambda value: lax.ppermute(value, axis, pairs)


core_swap = toward("core", NC, 1)
hi_swap = toward("x_hi", NX, 1)


def together(*values):
    return lax.optimization_barrier(values)


def dot(a, b):
    return jnp.dot(a, b, preferred_element_type=f32)


def reduce_y(partial):
    return [partial[:, 0]] + [toward("y", NY, -dy)(partial[:, dy]) for dy in (2, 1, 3)]


def add(parts):
    total = parts[0].astype(f32)
    for part in parts[1:]:
        total = total + part.astype(f32)
    return total


def attention_kernel(info_ref, both_ref, read_ref, kv_ref, grad_ref, tan_ref, sums_ref, keys_ref, values_ref):
    places, sides, part_rows, columns = read_ref.shape
    seqs = kv_ref.shape[0]
    rows = sides * part_rows
    chunks = both_ref.shape[0] // rows
    pairs = columns // LANES
    per_seq = places // seqs
    scale = f32(HD**-0.5)
    nt = (((1,), (1,)), ((), ()))
    low = lax.broadcasted_iota(jnp.int32, (kv_ref.shape[1], LANES), 1) < HD
    for s in range(seqs):
        kv = kv_ref[s]
        turned = pltpu.roll(kv, HD, 1)
        keys_ref[s] = jnp.concatenate([jnp.where(low, kv, 0.0), jnp.where(low, 0.0, turned)]).astype(bf16)
        values_ref[s] = jnp.concatenate([jnp.where(low, turned, 0.0), jnp.where(low, 0.0, kv)]).astype(bf16)
    lane = lax.broadcasted_iota(jnp.int32, (part_rows, LANES), 1)
    row = lax.broadcasted_iota(jnp.int32, (part_rows, LANES), 0)
    out_lane = lax.broadcasted_iota(jnp.int32, (1, LANES), 1)
    core = info_ref[chunks + seqs]
    stack = lambda blocks: jnp.concatenate(blocks, axis=0)
    column = lambda pair: slice(pair * LANES, (pair + 1) * LANES)
    sums = jnp.zeros((1, LANES), f32)
    for k in range(chunks):
        here = pl.ds(k * rows, rows)
        place = info_ref[k]
        seq = place // per_seq
        length = info_ref[chunks + seq]
        keys, values = keys_ref[seq], values_ref[seq]
        allowed, read = [], []
        for side in range(sides):
            position = ((place % per_seq * sides + side) * NC + core) * part_rows + row
            allowed.append(lane <= jnp.minimum(position, length - 1))
            live = position[:, :1] < length
            read.append(jnp.where(live, read_ref[place, side], 0.0))
        read = stack(read).astype(bf16)
        allowed = stack(allowed * pairs)
        both = both_ref[here, :].astype(bf16)
        both = lax.dot_general(
            stack([both[:, column(p)] for p in range(2 * pairs)]), keys, nt, preferred_element_type=f32
        )
        gain2 = lax.dot_general(
            stack([read[:, column(p)] for p in range(pairs)]), values, nt, preferred_element_type=f32
        )
        scores2, slope2 = both[: pairs * rows] * scale, both[pairs * rows :] * scale
        first, second = [], []
        logp = jnp.zeros((pairs * rows, 1), f32)
        logp_tan = jnp.zeros((pairs * rows, 1), f32)
        for head in range(2):
            part = column(head)
            scores = jnp.where(allowed, scores2[:, part], f32(-1e30))
            slope, gain = slope2[:, part], gain2[:, part]
            weights = jnp.exp(scores - jnp.max(scores, axis=1, keepdims=True))
            probs = weights / jnp.sum(weights, axis=1, keepdims=True)
            mean_gain = jnp.sum(probs * gain, axis=1, keepdims=True)
            mean_slope = jnp.sum(probs * slope, axis=1, keepdims=True)
            lean = gain - mean_gain
            pull = probs * (slope - mean_slope)
            mean_tan = jnp.sum(pull * lean, axis=1, keepdims=True)
            first.append((probs * lean).astype(bf16))
            second.append((pull * lean - probs * mean_tan).astype(bf16))
            logp = logp + mean_gain
            logp_tan = logp_tan + mean_tan
        out = dot(stack([jnp.concatenate(first, axis=1), jnp.concatenate(second, axis=1)]), keys) * scale
        for p in range(pairs):
            grad_ref[here, column(p)] = out[p * rows : (p + 1) * rows]
            tan_ref[here, column(p)] = out[(pairs + p) * rows : (pairs + p + 1) * rows]
        sums = sums + jnp.where(out_lane == seq, jnp.sum(logp), f32(0))
        sums = sums + jnp.where(out_lane == seq + LANES // 2, jnp.sum(logp_tan), f32(0))
    sums_ref[...] = sums


def attention(info, both, read, kv):
    rows, columns = both.shape[0], read.shape[-1]
    vmem = pl.BlockSpec(memory_space=pltpu.VMEM)
    return pl.pallas_call(
        attention_kernel,
        out_shape=(
            jax.ShapeDtypeStruct((rows, columns), f32),
            jax.ShapeDtypeStruct((rows, columns), f32),
            jax.ShapeDtypeStruct((1, LANES), f32),
        ),
        in_specs=[pl.BlockSpec(memory_space=pltpu.SMEM)] + [vmem] * 3,
        out_specs=(vmem, vmem, vmem),
        scratch_shapes=[pltpu.VMEM((kv.shape[0], 2 * kv.shape[1], LANES), bf16)] * 2,
        compiler_params=pltpu.CompilerParams(vmem_limit_bytes=12 * 1024 * 1024),
    )(info, both, read, kv)


def combine_kernel(chunks, seqs, info_ref, margin_ref, spread_ref, grad_ref, tan_ref, out_ref):
    total = jnp.sum(spread_ref[...], axis=0, keepdims=True)
    lane = lax.broadcasted_iota(jnp.int32, (1, LANES), 1)
    at = lambda i: jnp.sum(jnp.where(lane == i, total, f32(0)), axis=1, keepdims=True)
    coeffs = []
    for p in range(seqs // 2):
        margin = pair_beta * (at(2 * p) - at(2 * p + 1) - margin_ref[p])
        margin_tan = pair_beta * (at(LANES // 2 + 2 * p) - at(LANES // 2 + 2 * p + 1))
        sure, unsure = jax.nn.sigmoid(margin), jax.nn.sigmoid(-margin)
        slope = -pair_beta * unsure
        bend = pair_beta * unsure * sure * margin_tan
        coeffs += [(slope, bend), (-slope, -bend)]
    rows = grad_ref.shape[0] // chunks
    per_seq = NZ // seqs
    for k in range(chunks):
        seq = info_ref[k] // per_seq
        coeff, coeff_tan = coeffs[0]
        for s in range(1, seqs):
            coeff = jnp.where(seq == s, coeffs[s][0], coeff)
            coeff_tan = jnp.where(seq == s, coeffs[s][1], coeff_tan)
        here = pl.ds(k * rows, rows)
        out_ref[here, :] = coeff_tan * grad_ref[here, :] + coeff * tan_ref[here, :]


def combine(info, ref_margin, spread, grad, tan, seqs):
    vmem, smem = pl.BlockSpec(memory_space=pltpu.VMEM), pl.BlockSpec(memory_space=pltpu.SMEM)
    return pl.pallas_call(
        functools.partial(combine_kernel, len(CHUNKS), seqs),
        out_shape=jax.ShapeDtypeStruct(grad.shape, f32),
        in_specs=[smem, smem, vmem, vmem, vmem],
        out_specs=vmem,
        compiler_params=pltpu.CompilerParams(vmem_limit_bytes=6 * 1024 * 1024),
    )(info, ref_margin, spread, grad, tan)


def shards(hidden_in, norm_gain, query_weight, probe, key_values, readout, lengths, ref_margin):
    iy, ix, iz, ic = (lax.axis_index(a) for a in ("y", "x_hi", "z", "core"))
    tensor = ("z", "x_lo", "core")
    rows_here, width = hidden_in.shape
    feats, columns = query_weight.shape

    wide = hidden_in.astype(f32)
    stats = jnp.mean(wide * wide, axis=1, keepdims=True)
    normed = (wide * lax.rsqrt(stats + norm_epsilon) * norm_gain.astype(f32)).astype(bf16)

    other_q, other_t = core_swap(query_weight), core_swap(probe)
    sides = normed.reshape(rows_here, DP, feats).swapaxes(0, 1)
    sides = jnp.broadcast_to(sides[:, None], (DP, NL, rows_here, feats))
    first = lax.all_to_all(
        sides.reshape(DP * NL, rows_here, feats), ("y", "x_hi", "x_lo"), split_axis=0, concat_axis=0, tiled=True
    )
    first = first.reshape(NY, NX, -1, feats)
    first = lax.dynamic_slice_in_dim(jnp.concatenate([first, first]), iy, NY, 0)
    first = lax.dynamic_slice_in_dim(jnp.concatenate([first, first[:, :1]], axis=1), ix, NX, 1)
    first = first.reshape(DP * NL, rows_here, feats)
    chunk = {}
    chunk[0], other_q, other_t = together(first, other_q, other_t)

    seqs = lengths.shape[0] * 2
    seq_len = NZ // seqs * NL * NC * rows_here
    up, down = toward("z", NZ, -1), toward("z", NZ, 1)

    def multiply(group):
        rows = jnp.concatenate([chunk[k] for k in group]).reshape(-1, feats)
        return dot(rows, weights).astype(bf16).reshape(len(group), NY, NX, NL * rows_here, 4 * columns)

    chunk[1], chunk[-1] = down(chunk[0]), up(chunk[0])
    heads_kv, _ = together(key_values, chunk[0])
    heads_kv = heads_kv.reshape(rows_here, KVH, 2 * HD).swapaxes(0, 1)
    heads_kv = jnp.broadcast_to(heads_kv[:, None], (KVH, NL * NC, rows_here, 2 * HD))
    kv = lax.all_to_all(
        heads_kv.reshape(NZ * NL * NC, rows_here, 2 * HD), tensor, split_axis=0, concat_axis=0, tiled=True
    )
    weights = jnp.concatenate([query_weight, other_q, probe, other_t], axis=1)
    moved_0 = reduce_y(multiply((0,)))
    chunk[1], chunk[-1], kv, weights, *moved_0 = together(chunk[1], chunk[-1], kv, weights, *moved_0)
    chunk[2], chunk[-2] = down(chunk[1]), up(chunk[-1])
    moved_1 = reduce_y(multiply((1, -1)))
    total = add(moved_0)
    chunk[2], chunk[-2], total, *moved_1 = together(chunk[2], chunk[-2], total, *moved_1)
    chunk[3], chunk[-3] = down(chunk[2]), up(chunk[-2])
    moved_2 = reduce_y(multiply((2, -2)))
    total = jnp.concatenate([total, add(moved_1)])
    kv = kv.reshape(seqs, seq_len, 2 * HD).astype(f32)
    read = readout.reshape(NZ, NL, NC, rows_here, columns)
    mine = lax.dynamic_index_in_dim(read, ic, 2, False)
    theirs = lax.dynamic_index_in_dim(read, 1 - ic, 2, False)
    chunk[3], chunk[-3], total, kv, mine, theirs, *moved_2 = together(
        chunk[3], chunk[-3], total, kv, mine, theirs, *moved_2
    )
    half = DP * NL // 2
    ends = down(chunk[3][:half]), up(chunk[-3][half:])
    moved_3 = reduce_y(multiply((3, -3)))
    total = jnp.concatenate([total, add(moved_2)])
    *ends, total, mine, theirs, _ = together(*ends, total, mine, theirs, moved_3[-1])
    chunk[4] = jnp.concatenate(ends)
    read = jnp.concatenate([mine, core_swap(theirs)], axis=-1).astype(f32)
    info = jnp.concatenate([(iz + jnp.array(CHUNKS, jnp.int32) + NZ) % NZ, lengths.reshape(seqs), ic[None]])
    moved_4 = reduce_y(multiply((4,)))
    total = jnp.concatenate([total, add(moved_3)])
    cross = hi_swap(total[:, 1].astype(bf16))
    cross, total, read, *moved_4 = together(cross, total, read, *moved_4)
    last = add(moved_4)
    last = last[:, 0] + hi_swap(last[:, 1].astype(bf16)).astype(f32)
    projected = jnp.concatenate([total[:, 0] + cross.astype(f32), last]).reshape(-1, 4 * columns)
    normed_all = jnp.stack([chunk[k].reshape(DP, -1, feats) for k in CHUNKS], axis=1)

    grad, tan, sums = attention(info, projected, read, kv)
    spread = jnp.broadcast_to(sums[None], (NZ * NL * NC, 1, LANES))
    spread = lax.all_to_all(spread, tensor, split_axis=0, concat_axis=0, tiled=True).reshape(-1, LANES)
    hess_rows = combine(info, ref_margin, spread, grad, tan, seqs).astype(bf16)

    here, there = hess_rows[:, :columns], hess_rows[:, columns:]
    y_gather = lambda v: [v] + [toward("y", NY, dy)(v) for dy in (1, 2, 3)]
    there_x = hi_swap(there)
    here_y = y_gather(here)
    there_x, *here_y = together(there_x, *here_y)
    here_y = jnp.stack(here_y)
    here_all = hi_swap(here_y)
    there_all = y_gather(jnp.stack([there, there_x]))
    here_all, here_y, *there_all = together(here_all, here_y, *there_all)
    hess_all = jnp.concatenate([jnp.stack([here_y, here_all], axis=1), jnp.stack(there_all)], axis=-1)
    outer = lax.dot_general(
        normed_all.reshape(-1, feats),
        hess_all.reshape(-1, 2 * columns),
        (((0,), (0,)), ((), ())),
        preferred_element_type=f32,
    )
    return outer[:, :columns] + core_swap(outer[:, columns:].astype(bf16)).astype(f32)


def solution(mesh):
    fine = Mesh(
        mesh.devices.reshape(NY, NX, NZ, NL, NC), ("y", "x_hi", "z", "x_lo", "core")
    )
    dp, tensor = ("y", "x_hi"), ("z", "x_lo", "core")
    return jax.shard_map(
        shards,
        mesh=fine,
        in_specs=(
            P(dp + tensor, None),
            P(),
            P(dp, tensor),
            P(dp, tensor),
            P(dp + tensor, None),
            P(dp, tensor),
            P(dp, None),
            P(dp),
        ),
        out_specs=P(dp, tensor),
        check_vma=False,
    )
```

```python
import functools

import jax
import jax.numpy as jnp
from jax import lax
from jax.experimental import pallas as pl
from jax.experimental.pallas import tpu as pltpu
from jax.sharding import Mesh
from jax.sharding import PartitionSpec as P

HD = 64
KVH = 8
NY, NX, NZ, NL, NC = 4, 2, 8, 2, 2
DP = NY * NX

pair_beta = 0.5
norm_epsilon = 1e-05

bf16 = jnp.bfloat16
f32 = jnp.float32
CHUNKS = (0, 1, -1, 2, -2, 3, -3, 4)
LANES = 128


def toward(axis, size, shift):
    pairs = [((i + shift) % size, i) for i in range(size)]
    return lambda value: lax.ppermute(value, axis, pairs)


core_swap = toward("core", NC, 1)
hi_swap = toward("x_hi", NX, 1)


def together(*values):
    return lax.optimization_barrier(values)


def dot(a, b):
    return jnp.dot(a, b, preferred_element_type=f32)


def reduce_y(partial):
    return [partial[:, 0]] + [toward("y", NY, -dy)(partial[:, dy]) for dy in (2, 1, 3)]


def add(parts):
    total = parts[0].astype(f32)
    for part in parts[1:]:
        total = total + part.astype(f32)
    return total


def attention_kernel(info_ref, both_ref, read_ref, kv_ref, grad_ref, tan_ref, sums_ref, keys_ref, values_ref):
    places, sides, part_rows, columns = read_ref.shape
    seqs = kv_ref.shape[0]
    rows = sides * part_rows
    chunks = both_ref.shape[0] // rows
    pairs = columns // LANES
    per_seq = places // seqs
    scale = f32(HD**-0.5)
    nt = (((1,), (1,)), ((), ()))
    low = lax.broadcasted_iota(jnp.int32, (kv_ref.shape[1], LANES), 1) < HD
    for s in range(seqs):
        kv = kv_ref[s]
        turned = pltpu.roll(kv, HD, 1)
        keys_ref[s] = jnp.concatenate([jnp.where(low, kv, 0.0), jnp.where(low, 0.0, turned)]).astype(bf16)
        values_ref[s] = jnp.concatenate([jnp.where(low, turned, 0.0), jnp.where(low, 0.0, kv)]).astype(bf16)
    lane = lax.broadcasted_iota(jnp.int32, (part_rows, LANES), 1)
    row = lax.broadcasted_iota(jnp.int32, (part_rows, LANES), 0)
    out_lane = lax.broadcasted_iota(jnp.int32, (1, LANES), 1)
    core = info_ref[chunks + seqs]
    stack = lambda blocks: jnp.concatenate(blocks, axis=0)
    column = lambda pair: slice(pair * LANES, (pair + 1) * LANES)
    sums = jnp.zeros((1, LANES), f32)
    for k in range(chunks):
        here = pl.ds(k * rows, rows)
        place = info_ref[k]
        seq = place // per_seq
        length = info_ref[chunks + seq]
        keys, values = keys_ref[seq], values_ref[seq]
        allowed, read = [], []
        for side in range(sides):
            position = ((place % per_seq * sides + side) * NC + core) * part_rows + row
            allowed.append(lane <= jnp.minimum(position, length - 1))
            live = position[:, :1] < length
            read.append(jnp.where(live, read_ref[place, side], 0.0))
        read = stack(read).astype(bf16)
        allowed = stack(allowed * pairs)
        both = both_ref[here, :].astype(bf16)
        both = lax.dot_general(
            stack([both[:, column(p)] for p in range(2 * pairs)]), keys, nt, preferred_element_type=f32
        )
        gain2 = lax.dot_general(
            stack([read[:, column(p)] for p in range(pairs)]), values, nt, preferred_element_type=f32
        )
        scores2, slope2 = both[: pairs * rows] * scale, both[pairs * rows :] * scale
        first, second = [], []
        logp = jnp.zeros((pairs * rows, 1), f32)
        logp_tan = jnp.zeros((pairs * rows, 1), f32)
        for head in range(2):
            part = column(head)
            scores = jnp.where(allowed, scores2[:, part], f32(-1e30))
            slope, gain = slope2[:, part], gain2[:, part]
            weights = jnp.exp(scores - jnp.max(scores, axis=1, keepdims=True))
            probs = weights / jnp.sum(weights, axis=1, keepdims=True)
            mean_gain = jnp.sum(probs * gain, axis=1, keepdims=True)
            mean_slope = jnp.sum(probs * slope, axis=1, keepdims=True)
            lean = gain - mean_gain
            pull = probs * (slope - mean_slope)
            mean_tan = jnp.sum(pull * lean, axis=1, keepdims=True)
            first.append((probs * lean).astype(bf16))
            second.append((pull * lean - probs * mean_tan).astype(bf16))
            logp = logp + mean_gain
            logp_tan = logp_tan + mean_tan
        out = dot(stack([jnp.concatenate(first, axis=1), jnp.concatenate(second, axis=1)]), keys) * scale
        for p in range(pairs):
            grad_ref[here, column(p)] = out[p * rows : (p + 1) * rows]
            tan_ref[here, column(p)] = out[(pairs + p) * rows : (pairs + p + 1) * rows]
        sums = sums + jnp.where(out_lane == seq, jnp.sum(logp), f32(0))
        sums = sums + jnp.where(out_lane == seq + LANES // 2, jnp.sum(logp_tan), f32(0))
    sums_ref[...] = sums


def attention(info, both, read, kv):
    rows, columns = both.shape[0], read.shape[-1]
    vmem = pl.BlockSpec(memory_space=pltpu.VMEM)
    return pl.pallas_call(
        attention_kernel,
        out_shape=(
            jax.ShapeDtypeStruct((rows, columns), f32),
            jax.ShapeDtypeStruct((rows, columns), f32),
            jax.ShapeDtypeStruct((1, LANES), f32),
        ),
        in_specs=[pl.BlockSpec(memory_space=pltpu.SMEM)] + [vmem] * 3,
        out_specs=(vmem, vmem, vmem),
        scratch_shapes=[pltpu.VMEM((kv.shape[0], 2 * kv.shape[1], LANES), bf16)] * 2,
        compiler_params=pltpu.CompilerParams(vmem_limit_bytes=12 * 1024 * 1024),
    )(info, both, read, kv)


def combine_kernel(chunks, seqs, info_ref, margin_ref, spread_ref, grad_ref, grad_last_ref, tan_ref, tan_last_ref, out_ref):
    total = jnp.sum(spread_ref[...], axis=0, keepdims=True)
    lane = lax.broadcasted_iota(jnp.int32, (1, LANES), 1)
    at = lambda i: jnp.sum(jnp.where(lane == i, total, f32(0)), axis=1, keepdims=True)
    coeffs = []
    for p in range(seqs // 2):
        margin = pair_beta * (at(2 * p) - at(2 * p + 1) - margin_ref[p])
        margin_tan = pair_beta * (at(LANES // 2 + 2 * p) - at(LANES // 2 + 2 * p + 1))
        sure, unsure = jax.nn.sigmoid(margin), jax.nn.sigmoid(-margin)
        slope = -pair_beta * unsure
        bend = pair_beta * unsure * sure * margin_tan
        coeffs += [(slope, bend), (-slope, -bend)]
    rows = grad_last_ref.shape[0]
    per_seq = NZ // seqs
    for k in range(chunks):
        seq = info_ref[k] // per_seq
        coeff, coeff_tan = coeffs[0]
        for s in range(1, seqs):
            coeff = jnp.where(seq == s, coeffs[s][0], coeff)
            coeff_tan = jnp.where(seq == s, coeffs[s][1], coeff_tan)
        here = pl.ds(k * rows, rows)
        if k < chunks - 1:
            grad, tan = grad_ref[here, :], tan_ref[here, :]
        else:
            grad, tan = grad_last_ref[...], tan_last_ref[...]
        out_ref[here, :] = coeff_tan * grad + coeff * tan


def combine(info, ref_margin, spread, grad, tan, seqs):
    vmem, smem = pl.BlockSpec(memory_space=pltpu.VMEM), pl.BlockSpec(memory_space=pltpu.SMEM)
    return pl.pallas_call(
        functools.partial(combine_kernel, len(CHUNKS), seqs),
        out_shape=jax.ShapeDtypeStruct((grad[0].shape[0] + grad[1].shape[0], grad[0].shape[1]), f32),
        in_specs=[smem, smem, vmem] + [vmem] * 4,
        out_specs=vmem,
        compiler_params=pltpu.CompilerParams(vmem_limit_bytes=6 * 1024 * 1024),
    )(info, ref_margin, spread, *grad, *tan)


def shards(hidden_in, norm_gain, query_weight, probe, key_values, readout, lengths, ref_margin):
    iy, ix, iz, ic = (lax.axis_index(a) for a in ("y", "x_hi", "z", "core"))
    tensor = ("z", "x_lo", "core")
    rows_here, width = hidden_in.shape
    feats, columns = query_weight.shape

    wide = hidden_in.astype(f32)
    stats = jnp.mean(wide * wide, axis=1, keepdims=True)
    normed = (wide * lax.rsqrt(stats + norm_epsilon) * norm_gain.astype(f32)).astype(bf16)

    heads_kv, normed = together(key_values, normed)
    sides = normed.reshape(rows_here, DP, feats).swapaxes(0, 1)
    sides = jnp.broadcast_to(sides[:, None], (DP, NL, rows_here, feats))
    first = lax.all_to_all(
        sides.reshape(DP * NL, rows_here, feats), ("y", "x_hi", "x_lo"), split_axis=0, concat_axis=0, tiled=True
    )
    weights = jnp.concatenate([query_weight, core_swap(query_weight), probe, core_swap(probe)], axis=1)
    heads_kv = heads_kv.reshape(rows_here, KVH, 2 * HD).swapaxes(0, 1)
    heads_kv = jnp.broadcast_to(heads_kv[:, None], (KVH, NL * NC, rows_here, 2 * HD))
    kv = lax.all_to_all(
        heads_kv.reshape(NZ * NL * NC, rows_here, 2 * HD), tensor, split_axis=0, concat_axis=0, tiled=True
    )
    first, weights = together(first, weights)
    first = first.reshape(NY, NX, -1, feats)
    first = lax.dynamic_slice_in_dim(jnp.concatenate([first, first]), iy, NY, 0)
    first = lax.dynamic_slice_in_dim(jnp.concatenate([first, first[:, :1]], axis=1), ix, NX, 1)
    first = first.reshape(DP * NL, rows_here, feats)
    chunk = {}
    (chunk[0],) = together(first)

    seqs = lengths.shape[0] * 2
    seq_len = NZ // seqs * NL * NC * rows_here
    up, down = toward("z", NZ, -1), toward("z", NZ, 1)

    def multiply(group):
        rows = jnp.concatenate([chunk[k] for k in group]).reshape(-1, feats)
        return dot(rows, weights).astype(bf16).reshape(len(group), NY, NX, NL * rows_here, 4 * columns)

    chunk[1], chunk[-1] = down(chunk[0]), up(chunk[0])
    moved_0 = reduce_y(multiply((0,)))
    chunk[1], chunk[-1], kv, *moved_0 = together(chunk[1], chunk[-1], kv, *moved_0)
    chunk[2], chunk[-2] = down(chunk[1]), up(chunk[-1])
    moved_1 = reduce_y(multiply((1, -1)))
    total = add(moved_0)
    chunk[2], chunk[-2], total, *moved_1 = together(chunk[2], chunk[-2], total, *moved_1)
    chunk[3], chunk[-3] = down(chunk[2]), up(chunk[-2])
    moved_2 = reduce_y(multiply((2, -2)))
    total = jnp.concatenate([total, add(moved_1)])
    kv = kv.reshape(seqs, seq_len, 2 * HD).astype(f32)
    read = readout.reshape(NZ, NL, NC, rows_here, columns)
    mine = lax.dynamic_index_in_dim(read, ic, 2, False)
    theirs = lax.dynamic_index_in_dim(read, 1 - ic, 2, False)
    chunk[3], chunk[-3], total, kv, mine, theirs, *moved_2 = together(
        chunk[3], chunk[-3], total, kv, mine, theirs, *moved_2
    )
    half = DP * NL // 2
    ends = down(chunk[3][:half]), up(chunk[-3][half:])
    moved_3 = reduce_y(multiply((3, -3)))
    total = jnp.concatenate([total, add(moved_2)])
    *ends, total, mine, theirs = together(*ends, total, mine, theirs)
    chunk[4] = jnp.concatenate(ends)
    read = jnp.concatenate([mine, core_swap(theirs)], axis=-1).astype(f32)
    info = jnp.concatenate([(iz + jnp.array(CHUNKS, jnp.int32) + NZ) % NZ, lengths.reshape(seqs), ic[None]])
    moved_4 = reduce_y(multiply((4,)))
    total = jnp.concatenate([total, add(moved_3)])
    cross = hi_swap(total[:, 1].astype(bf16))
    cross, total, read, *moved_4 = together(cross, total, read, *moved_4)
    early = (total[:, 0] + cross.astype(f32)).reshape(-1, 4 * columns)
    last = add(moved_4)
    last = (last[:, 0] + hi_swap(last[:, 1].astype(bf16)).astype(f32)).reshape(-1, 4 * columns)
    normed_all = jnp.stack([chunk[k].reshape(DP, -1, feats) for k in CHUNKS], axis=1)

    places, rest = info[: len(CHUNKS)], info[len(CHUNKS) :]
    grad, tan, sums = attention(jnp.concatenate([places[:-1], rest]), early, read, kv)
    grad_last, tan_last, sums_last = attention(jnp.concatenate([places[-1:], rest]), last, read, kv)
    spread = jnp.broadcast_to((sums + sums_last)[None], (NZ * NL * NC, 1, LANES))
    spread = lax.all_to_all(spread, tensor, split_axis=0, concat_axis=0, tiled=True).reshape(-1, LANES)
    spread, normed_all = together(spread, normed_all)
    hess_rows = combine(info, ref_margin, spread, (grad, grad_last), (tan, tan_last), seqs).astype(bf16)

    here, there = hess_rows[:, :columns], hess_rows[:, columns:]
    y_gather = lambda v: [v] + [toward("y", NY, dy)(v) for dy in (1, 2, 3)]
    there_x = hi_swap(there)
    here_y = y_gather(here)
    there_x, *here_y = together(there_x, *here_y)
    here_y = jnp.stack(here_y)
    here_all = hi_swap(here_y)
    there_all = y_gather(jnp.stack([there, there_x]))
    here_all, here_y, *there_all = together(here_all, here_y, *there_all)
    hess_all = jnp.concatenate([jnp.stack([here_y, here_all], axis=1), jnp.stack(there_all)], axis=-1)
    outer = lax.dot_general(
        normed_all.reshape(-1, feats),
        hess_all.reshape(-1, 2 * columns),
        (((0,), (0,)), ((), ())),
        preferred_element_type=f32,
    )
    return outer[:, :columns] + core_swap(outer[:, columns:].astype(bf16)).astype(f32)


def solution(mesh):
    fine = Mesh(
        mesh.devices.reshape(NY, NX, NZ, NL, NC), ("y", "x_hi", "z", "x_lo", "core")
    )
    dp, tensor = ("y", "x_hi"), ("z", "x_lo", "core")
    return jax.shard_map(
        shards,
        mesh=fine,
        in_specs=(
            P(dp + tensor, None),
            P(),
            P(dp, tensor),
            P(dp, tensor),
            P(dp + tensor, None),
            P(dp, tensor),
            P(dp, None),
            P(dp),
        ),
        out_specs=P(dp, tensor),
        check_vma=False,
    )
```

```python
import functools

import jax
import jax.numpy as jnp
from jax import lax
from jax.experimental import pallas as pl
from jax.experimental.pallas import tpu as pltpu
from jax.sharding import Mesh
from jax.sharding import PartitionSpec as P

HD = 64
KVH = 8
NY, NX, NZ, NL, NC = 4, 2, 8, 2, 2
DP = NY * NX

pair_beta = 0.5
norm_epsilon = 1e-05

bf16 = jnp.bfloat16
f32 = jnp.float32
CHUNKS = (0, 1, -1, 2, -2, 3, -3, 4)
LANES = 128


def toward(axis, size, shift):
    pairs = [((i + shift) % size, i) for i in range(size)]
    return lambda value: lax.ppermute(value, axis, pairs)


core_swap = toward("core", NC, 1)
hi_swap = toward("x_hi", NX, 1)


def together(*values):
    return lax.optimization_barrier(values)


def dot(a, b):
    return jnp.dot(a, b, preferred_element_type=f32)


def reduce_y(partial):
    return [partial[:, 0]] + [toward("y", NY, -dy)(partial[:, dy]) for dy in (2, 1, 3)]


def add(parts):
    total = parts[0].astype(f32)
    for part in parts[1:]:
        total = total + part.astype(f32)
    return total


def attention_kernel(info_ref, both_ref, read_ref, kv_ref, grad_ref, tan_ref, sums_ref, keys_ref, values_ref):
    places, sides, part_rows, columns = read_ref.shape
    seqs = kv_ref.shape[0]
    rows = sides * part_rows
    chunks = both_ref.shape[0] // rows
    pairs = columns // LANES
    per_seq = places // seqs
    scale = f32(HD**-0.5)
    nt = (((1,), (1,)), ((), ()))
    low = lax.broadcasted_iota(jnp.int32, (kv_ref.shape[1], LANES), 1) < HD
    for s in range(seqs):
        kv = kv_ref[s]
        turned = pltpu.roll(kv, HD, 1)
        keys_ref[s] = jnp.concatenate([jnp.where(low, kv, 0.0), jnp.where(low, 0.0, turned)]).astype(bf16)
        values_ref[s] = jnp.concatenate([jnp.where(low, turned, 0.0), jnp.where(low, 0.0, kv)]).astype(bf16)
    lane = lax.broadcasted_iota(jnp.int32, (part_rows, LANES), 1)
    row = lax.broadcasted_iota(jnp.int32, (part_rows, LANES), 0)
    out_lane = lax.broadcasted_iota(jnp.int32, (1, LANES), 1)
    core = info_ref[chunks + seqs]
    stack = lambda blocks: jnp.concatenate(blocks, axis=0)
    column = lambda pair: slice(pair * LANES, (pair + 1) * LANES)
    sums = jnp.zeros((1, LANES), f32)
    for k in range(chunks):
        here = pl.ds(k * rows, rows)
        place = info_ref[k]
        seq = place // per_seq
        length = info_ref[chunks + seq]
        keys, values = keys_ref[seq], values_ref[seq]
        allowed, read = [], []
        for side in range(sides):
            position = ((place % per_seq * sides + side) * NC + core) * part_rows + row
            allowed.append(lane <= jnp.minimum(position, length - 1))
            live = position[:, :1] < length
            read.append(jnp.where(live, read_ref[place, side], 0.0))
        read = stack(read).astype(bf16)
        allowed = stack(allowed * pairs)
        both = both_ref[here, :].astype(bf16)
        both = lax.dot_general(
            stack([both[:, column(p)] for p in range(2 * pairs)]), keys, nt, preferred_element_type=f32
        )
        gain2 = lax.dot_general(
            stack([read[:, column(p)] for p in range(pairs)]), values, nt, preferred_element_type=f32
        )
        scores2, slope2 = both[: pairs * rows] * scale, both[pairs * rows :] * scale
        first, second = [], []
        logp = jnp.zeros((pairs * rows, 1), f32)
        logp_tan = jnp.zeros((pairs * rows, 1), f32)
        for head in range(2):
            part = column(head)
            scores = jnp.where(allowed, scores2[:, part], f32(-1e30))
            slope, gain = slope2[:, part], gain2[:, part]
            weights = jnp.exp(scores - jnp.max(scores, axis=1, keepdims=True))
            probs = weights / jnp.sum(weights, axis=1, keepdims=True)
            mean_gain = jnp.sum(probs * gain, axis=1, keepdims=True)
            mean_slope = jnp.sum(probs * slope, axis=1, keepdims=True)
            lean = gain - mean_gain
            pull = probs * (slope - mean_slope)
            mean_tan = jnp.sum(pull * lean, axis=1, keepdims=True)
            first.append((probs * lean).astype(bf16))
            second.append((pull * lean - probs * mean_tan).astype(bf16))
            logp = logp + mean_gain
            logp_tan = logp_tan + mean_tan
        out = dot(stack([jnp.concatenate(first, axis=1), jnp.concatenate(second, axis=1)]), keys) * scale
        for p in range(pairs):
            grad_ref[here, column(p)] = out[p * rows : (p + 1) * rows]
            tan_ref[here, column(p)] = out[(pairs + p) * rows : (pairs + p + 1) * rows]
        sums = sums + jnp.where(out_lane == seq, jnp.sum(logp), f32(0))
        sums = sums + jnp.where(out_lane == seq + LANES // 2, jnp.sum(logp_tan), f32(0))
    sums_ref[...] = sums


def attention(info, both, read, kv):
    rows, columns = both.shape[0], read.shape[-1]
    vmem = pl.BlockSpec(memory_space=pltpu.VMEM)
    return pl.pallas_call(
        attention_kernel,
        out_shape=(
            jax.ShapeDtypeStruct((rows, columns), f32),
            jax.ShapeDtypeStruct((rows, columns), f32),
            jax.ShapeDtypeStruct((1, LANES), f32),
        ),
        in_specs=[pl.BlockSpec(memory_space=pltpu.SMEM)] + [vmem] * 3,
        out_specs=(vmem, vmem, vmem),
        scratch_shapes=[pltpu.VMEM((kv.shape[0], 2 * kv.shape[1], LANES), bf16)] * 2,
        compiler_params=pltpu.CompilerParams(vmem_limit_bytes=12 * 1024 * 1024),
    )(info, both, read, kv)


def combine_kernel(chunks, seqs, info_ref, margin_ref, spread_ref, grad_ref, tan_ref, out_ref):
    total = jnp.sum(spread_ref[...], axis=0, keepdims=True)
    lane = lax.broadcasted_iota(jnp.int32, (1, LANES), 1)
    at = lambda i: jnp.sum(jnp.where(lane == i, total, f32(0)), axis=1, keepdims=True)
    coeffs = []
    for p in range(seqs // 2):
        margin = pair_beta * (at(2 * p) - at(2 * p + 1) - margin_ref[p])
        margin_tan = pair_beta * (at(LANES // 2 + 2 * p) - at(LANES // 2 + 2 * p + 1))
        sure, unsure = jax.nn.sigmoid(margin), jax.nn.sigmoid(-margin)
        slope = -pair_beta * unsure
        bend = pair_beta * unsure * sure * margin_tan
        coeffs += [(slope, bend), (-slope, -bend)]
    rows = grad_ref.shape[0] // chunks
    per_seq = NZ // seqs
    for k in range(chunks):
        seq = info_ref[k] // per_seq
        coeff, coeff_tan = coeffs[0]
        for s in range(1, seqs):
            coeff = jnp.where(seq == s, coeffs[s][0], coeff)
            coeff_tan = jnp.where(seq == s, coeffs[s][1], coeff_tan)
        here = pl.ds(k * rows, rows)
        out_ref[here, :] = coeff_tan * grad_ref[here, :] + coeff * tan_ref[here, :]


def combine(info, ref_margin, spread, grad, tan, seqs):
    vmem, smem = pl.BlockSpec(memory_space=pltpu.VMEM), pl.BlockSpec(memory_space=pltpu.SMEM)
    return pl.pallas_call(
        functools.partial(combine_kernel, len(CHUNKS), seqs),
        out_shape=jax.ShapeDtypeStruct(grad.shape, f32),
        in_specs=[smem, smem, vmem, vmem, vmem],
        out_specs=vmem,
        compiler_params=pltpu.CompilerParams(vmem_limit_bytes=6 * 1024 * 1024),
    )(info, ref_margin, spread, grad, tan)


def shards(hidden_in, norm_gain, query_weight, probe, key_values, readout, lengths, ref_margin):
    iy, ix, iz, ic = (lax.axis_index(a) for a in ("y", "x_hi", "z", "core"))
    tensor = ("z", "x_lo", "core")
    rows_here, width = hidden_in.shape
    feats, columns = query_weight.shape

    wide = hidden_in.astype(f32)
    stats = jnp.mean(wide * wide, axis=1, keepdims=True)
    normed = (wide * lax.rsqrt(stats + norm_epsilon) * norm_gain.astype(f32)).astype(bf16)

    sides = normed.reshape(rows_here, DP, feats).swapaxes(0, 1)
    sides = jnp.broadcast_to(sides[:, None], (DP, NL, rows_here, feats))
    first = lax.all_to_all(
        sides.reshape(DP * NL, rows_here, feats), ("y", "x_hi", "x_lo"), split_axis=0, concat_axis=0, tiled=True
    )
    weights = jnp.concatenate([query_weight, core_swap(query_weight), probe, core_swap(probe)], axis=1)
    first, weights = together(first, weights)
    first = first.reshape(NY, NX, -1, feats)
    first = lax.dynamic_slice_in_dim(jnp.concatenate([first, first]), iy, NY, 0)
    first = lax.dynamic_slice_in_dim(jnp.concatenate([first, first[:, :1]], axis=1), ix, NX, 1)
    first = first.reshape(DP * NL, rows_here, feats)
    chunk = {}
    (chunk[0],) = together(first)

    seqs = lengths.shape[0] * 2
    seq_len = NZ // seqs * NL * NC * rows_here
    up, down = toward("z", NZ, -1), toward("z", NZ, 1)

    def multiply(group):
        rows = jnp.concatenate([chunk[k] for k in group]).reshape(-1, feats)
        return dot(rows, weights).astype(bf16).reshape(len(group), NY, NX, NL * rows_here, 4 * columns)

    chunk[1], chunk[-1] = down(chunk[0]), up(chunk[0])
    heads_kv, _ = together(key_values, chunk[0])
    heads_kv = heads_kv.reshape(rows_here, KVH, 2 * HD).swapaxes(0, 1)
    heads_kv = jnp.broadcast_to(heads_kv[:, None], (KVH, NL * NC, rows_here, 2 * HD))
    kv = lax.all_to_all(
        heads_kv.reshape(NZ * NL * NC, rows_here, 2 * HD), tensor, split_axis=0, concat_axis=0, tiled=True
    )
    moved_0 = reduce_y(multiply((0,)))
    chunk[1], chunk[-1], kv, *moved_0 = together(chunk[1], chunk[-1], kv, *moved_0)
    chunk[2], chunk[-2] = down(chunk[1]), up(chunk[-1])
    moved_1 = reduce_y(multiply((1, -1)))
    total = add(moved_0)
    chunk[2], chunk[-2], total, *moved_1 = together(chunk[2], chunk[-2], total, *moved_1)
    chunk[3], chunk[-3] = down(chunk[2]), up(chunk[-2])
    moved_2 = reduce_y(multiply((2, -2)))
    total = jnp.concatenate([total, add(moved_1)])
    kv = kv.reshape(seqs, seq_len, 2 * HD).astype(f32)
    read = readout.reshape(NZ, NL, NC, rows_here, columns)
    mine = lax.dynamic_index_in_dim(read, ic, 2, False)
    theirs = lax.dynamic_index_in_dim(read, 1 - ic, 2, False)
    chunk[3], chunk[-3], total, kv, mine, theirs, *moved_2 = together(
        chunk[3], chunk[-3], total, kv, mine, theirs, *moved_2
    )
    half = DP * NL // 2
    ends = down(chunk[3][:half]), up(chunk[-3][half:])
    moved_3 = reduce_y(multiply((3, -3)))
    total = jnp.concatenate([total, add(moved_2)])
    *ends, total, mine, theirs = together(*ends, total, mine, theirs)
    chunk[4] = jnp.concatenate(ends)
    read = jnp.concatenate([mine, core_swap(theirs)], axis=-1).astype(f32)
    info = jnp.concatenate([(iz + jnp.array(CHUNKS, jnp.int32) + NZ) % NZ, lengths.reshape(seqs), ic[None]])
    moved_4 = reduce_y(multiply((4,)))
    total = jnp.concatenate([total, add(moved_3)])
    cross = hi_swap(total[:, 1].astype(bf16))
    cross, total, read, *moved_4 = together(cross, total, read, *moved_4)
    early = (total[:, 0] + cross.astype(f32)).reshape(-1, 4 * columns)
    last = add(moved_4)
    last = (last[:, 0] + hi_swap(last[:, 1].astype(bf16)).astype(f32)).reshape(-1, 4 * columns)
    normed_all = jnp.stack([chunk[k].reshape(DP, -1, feats) for k in CHUNKS], axis=1)

    projected = jnp.concatenate([early, last])
    grad, tan, sums = attention(info, projected, read, kv)
    spread = jnp.broadcast_to(sums[None], (NZ * NL * NC, 1, LANES))
    spread = lax.all_to_all(spread, tensor, split_axis=0, concat_axis=0, tiled=True).reshape(-1, LANES)
    spread, normed_all = together(spread, normed_all)
    hess_rows = combine(info, ref_margin, spread, grad, tan, seqs).astype(bf16)

    here, there = hess_rows[:, :columns], hess_rows[:, columns:]
    y_gather = lambda v: [v] + [toward("y", NY, dy)(v) for dy in (1, 2, 3)]
    there_x = hi_swap(there)
    here_y = y_gather(here)
    there_x, *here_y = together(there_x, *here_y)
    here_y = jnp.stack(here_y)
    here_all = hi_swap(here_y)
    there_all = y_gather(jnp.stack([there, there_x]))
    here_all, here_y, *there_all = together(here_all, here_y, *there_all)
    hess_all = jnp.concatenate([jnp.stack([here_y, here_all], axis=1), jnp.stack(there_all)], axis=-1)
    outer = lax.dot_general(
        normed_all.reshape(-1, feats),
        hess_all.reshape(-1, 2 * columns),
        (((0,), (0,)), ((), ())),
        preferred_element_type=f32,
    )
    return outer[:, :columns] + core_swap(outer[:, columns:].astype(bf16)).astype(f32)


def solution(mesh):
    fine = Mesh(
        mesh.devices.reshape(NY, NX, NZ, NL, NC), ("y", "x_hi", "z", "x_lo", "core")
    )
    dp, tensor = ("y", "x_hi"), ("z", "x_lo", "core")
    return jax.shard_map(
        shards,
        mesh=fine,
        in_specs=(
            P(dp + tensor, None),
            P(),
            P(dp, tensor),
            P(dp, tensor),
            P(dp + tensor, None),
            P(dp, tensor),
            P(dp, None),
            P(dp),
        ),
        out_specs=P(dp, tensor),
        check_vma=False,
    )
```

```python
import functools

import jax
import jax.numpy as jnp
from jax import lax
from jax.experimental import pallas as pl
from jax.experimental.pallas import tpu as pltpu
from jax.sharding import Mesh
from jax.sharding import PartitionSpec as P

HD = 64
KVH = 8
EARLY = 3
NY, NX, NZ, NL, NC = 4, 2, 8, 2, 2
DP = NY * NX

pair_beta = 0.5
norm_epsilon = 1e-05

bf16 = jnp.bfloat16
f32 = jnp.float32
CHUNKS = (0, 1, -1, 3, -3, 2, -2, 4)
LANES = 128


def toward(axis, size, shift):
    pairs = [((i + shift) % size, i) for i in range(size)]
    return lambda value: lax.ppermute(value, axis, pairs)


core_swap = toward("core", NC, 1)
hi_swap = toward("x_hi", NX, 1)
lo_swap = toward("x_lo", NL, 1)


def together(*values):
    return lax.optimization_barrier(values)


def dot(a, b):
    return jnp.dot(a, b, preferred_element_type=f32)


def reduce_y(partial):
    return [partial[:, :, 0]] + [toward("y", NY, -dy)(partial[:, :, dy]) for dy in (2, 1, 3)]


def scatter_y(partial, iy):
    major = jnp.moveaxis(partial, 2, 0)
    major = lax.dynamic_slice_in_dim(jnp.concatenate([major, major]), NY - iy, NY, 0)
    return lax.psum_scatter(major, "y", scatter_dimension=0, tiled=True)[0]


def add(parts):
    total = parts[0].astype(f32)
    for part in parts[1:]:
        total = total + part.astype(f32)
    return total


def attention_kernel(info_ref, both_ref, read_ref, kv_ref, grad_ref, tan_ref, sums_ref, keys_ref, values_ref):
    places, sides, part_rows, columns = read_ref.shape
    seqs = kv_ref.shape[0]
    rows = sides * part_rows
    chunks = both_ref.shape[0] // rows
    pairs = columns // LANES
    per_seq = places // seqs
    scale = f32(HD**-0.5)
    nt = (((1,), (1,)), ((), ()))
    low = lax.broadcasted_iota(jnp.int32, (kv_ref.shape[1], LANES), 1) < HD
    for s in range(seqs):
        kv = kv_ref[s]
        turned = pltpu.roll(kv, HD, 1)
        keys_ref[s] = jnp.concatenate([jnp.where(low, kv, 0.0), jnp.where(low, 0.0, turned)]).astype(bf16)
        values_ref[s] = jnp.concatenate([jnp.where(low, turned, 0.0), jnp.where(low, 0.0, kv)]).astype(bf16)
    lane = lax.broadcasted_iota(jnp.int32, (part_rows, LANES), 1)
    row = lax.broadcasted_iota(jnp.int32, (part_rows, LANES), 0)
    out_lane = lax.broadcasted_iota(jnp.int32, (1, LANES), 1)
    x_lo, core = info_ref[chunks + seqs], info_ref[chunks + seqs + 1]
    stack = lambda blocks: jnp.concatenate(blocks, axis=0)
    column = lambda pair: slice(pair * LANES, (pair + 1) * LANES)
    sums = jnp.zeros((1, LANES), f32)
    for k in range(chunks):
        here = pl.ds(k * rows, rows)
        place = info_ref[k]
        seq = place // per_seq
        length = info_ref[chunks + seq]
        keys, values = keys_ref[seq], values_ref[seq]
        allowed, read = [], []
        for side in (x_lo, 1 - x_lo):
            position = ((place % per_seq * sides + side) * NC + core) * part_rows + row
            allowed.append(lane <= jnp.minimum(position, length - 1))
            live = position[:, :1] < length
            read.append(jnp.where(live, read_ref[place, side], 0.0))
        read = stack(read).astype(bf16)
        allowed = stack(allowed * pairs)
        both = both_ref[here, :].astype(bf16)
        both = lax.dot_general(
            stack([both[:, column(p)] for p in range(2 * pairs)]), keys, nt, preferred_element_type=f32
        )
        gain2 = lax.dot_general(
            stack([read[:, column(p)] for p in range(pairs)]), values, nt, preferred_element_type=f32
        )
        scores2, slope2 = both[: pairs * rows] * scale, both[pairs * rows :] * scale
        first, second = [], []
        logp = jnp.zeros((pairs * rows, 1), f32)
        logp_tan = jnp.zeros((pairs * rows, 1), f32)
        for head in range(2):
            part = column(head)
            scores = jnp.where(allowed, scores2[:, part], f32(-1e30))
            slope, gain = slope2[:, part], gain2[:, part]
            weights = jnp.exp(scores - jnp.max(scores, axis=1, keepdims=True))
            probs = weights / jnp.sum(weights, axis=1, keepdims=True)
            mean_gain = jnp.sum(probs * gain, axis=1, keepdims=True)
            mean_slope = jnp.sum(probs * slope, axis=1, keepdims=True)
            lean = gain - mean_gain
            pull = probs * (slope - mean_slope)
            mean_tan = jnp.sum(pull * lean, axis=1, keepdims=True)
            first.append((probs * lean).astype(bf16))
            second.append((pull * lean - probs * mean_tan).astype(bf16))
            logp = logp + mean_gain
            logp_tan = logp_tan + mean_tan
        out = dot(stack([jnp.concatenate(first, axis=1), jnp.concatenate(second, axis=1)]), keys) * scale
        for p in range(pairs):
            grad_ref[here, column(p)] = out[p * rows : (p + 1) * rows]
            tan_ref[here, column(p)] = out[(pairs + p) * rows : (pairs + p + 1) * rows]
        sums = sums + jnp.where(out_lane == seq, jnp.sum(logp), f32(0))
        sums = sums + jnp.where(out_lane == seq + LANES // 2, jnp.sum(logp_tan), f32(0))
    sums_ref[...] = sums


def attention(info, both, read, kv):
    rows, columns = both.shape[0], read.shape[-1]
    vmem = pl.BlockSpec(memory_space=pltpu.VMEM)
    return pl.pallas_call(
        attention_kernel,
        out_shape=(
            jax.ShapeDtypeStruct((rows, columns), f32),
            jax.ShapeDtypeStruct((rows, columns), f32),
            jax.ShapeDtypeStruct((1, LANES), f32),
        ),
        in_specs=[pl.BlockSpec(memory_space=pltpu.SMEM)] + [vmem] * 3,
        out_specs=(vmem, vmem, vmem),
        scratch_shapes=[pltpu.VMEM((kv.shape[0], 2 * kv.shape[1], LANES), bf16)] * 2,
        compiler_params=pltpu.CompilerParams(vmem_limit_bytes=12 * 1024 * 1024),
    )(info, both, read, kv)


def combine_kernel(chunks, seqs, info_ref, margin_ref, spread_ref, grad_ref, tan_ref, out_ref):
    total = jnp.sum(spread_ref[...], axis=0, keepdims=True)
    lane = lax.broadcasted_iota(jnp.int32, (1, LANES), 1)
    at = lambda i: jnp.sum(jnp.where(lane == i, total, f32(0)), axis=1, keepdims=True)
    coeffs = []
    for p in range(seqs // 2):
        margin = pair_beta * (at(2 * p) - at(2 * p + 1) - margin_ref[p])
        margin_tan = pair_beta * (at(LANES // 2 + 2 * p) - at(LANES // 2 + 2 * p + 1))
        sure, unsure = jax.nn.sigmoid(margin), jax.nn.sigmoid(-margin)
        slope = -pair_beta * unsure
        bend = pair_beta * unsure * sure * margin_tan
        coeffs += [(slope, bend), (-slope, -bend)]
    rows = grad_ref.shape[0] // chunks
    per_seq = NZ // seqs
    for k in range(chunks):
        seq = info_ref[k] // per_seq
        coeff, coeff_tan = coeffs[0]
        for s in range(1, seqs):
            coeff = jnp.where(seq == s, coeffs[s][0], coeff)
            coeff_tan = jnp.where(seq == s, coeffs[s][1], coeff_tan)
        here = pl.ds(k * rows, rows)
        out_ref[here, :] = coeff_tan * grad_ref[here, :] + coeff * tan_ref[here, :]


def combine(info, ref_margin, spread, grad, tan, seqs):
    vmem, smem = pl.BlockSpec(memory_space=pltpu.VMEM), pl.BlockSpec(memory_space=pltpu.SMEM)
    return pl.pallas_call(
        functools.partial(combine_kernel, len(CHUNKS), seqs),
        out_shape=jax.ShapeDtypeStruct(grad.shape, f32),
        in_specs=[smem, smem, vmem, vmem, vmem],
        out_specs=vmem,
        compiler_params=pltpu.CompilerParams(vmem_limit_bytes=6 * 1024 * 1024),
    )(info, ref_margin, spread, grad, tan)


def shards(hidden_in, norm_gain, query_weight, probe, key_values, readout, lengths, ref_margin):
    iy, ix, iz, il, ic = (lax.axis_index(a) for a in ("y", "x_hi", "z", "x_lo", "core"))
    tensor = ("z", "x_lo", "core")
    rows_here, width = hidden_in.shape
    feats, columns = query_weight.shape

    wide = hidden_in.astype(f32)
    stats = jnp.mean(wide * wide, axis=1, keepdims=True)
    normed = (wide * lax.rsqrt(stats + norm_epsilon) * norm_gain.astype(f32)).astype(bf16)

    sides = normed.reshape(rows_here, DP, feats).swapaxes(0, 1)
    sides = jnp.broadcast_to(sides[:, None], (DP, NL, rows_here, feats))
    first = lax.all_to_all(
        sides.reshape(DP * NL, rows_here, feats), ("y", "x_hi", "x_lo"), split_axis=0, concat_axis=0, tiled=True
    )
    weights = jnp.concatenate([query_weight, core_swap(query_weight), probe, core_swap(probe)], axis=1)
    first, weights = together(first, weights)
    first = first.reshape(NY, NX, NL, rows_here, feats)
    first = lax.dynamic_slice_in_dim(jnp.concatenate([first, first]), iy, NY, 0)
    first = lax.dynamic_slice_in_dim(jnp.concatenate([first, first[:, :1]], axis=1), ix, NX, 1)
    first = lax.dynamic_slice_in_dim(jnp.concatenate([first, first[:, :, :1]], axis=2), il, NL, 2)
    first = first.reshape(DP, NL, rows_here, feats).swapaxes(0, 1).reshape(NL * DP, rows_here, feats)
    along, across = {}, {}
    along[0], across[0] = together(first[: DP + EARLY], first[DP + EARLY :])

    seqs = lengths.shape[0] * 2
    seq_len = NZ // seqs * NL * NC * rows_here
    up, down = toward("z", NZ, -1), toward("z", NZ, 1)

    def multiply(group):
        rows = jnp.concatenate([v for k in group for v in (along[k], across[k])]).reshape(-1, feats)
        return dot(rows, weights).astype(bf16).reshape(len(group), NL, NY, NX, rows_here, 4 * columns)

    def swap_rest(k):
        return lo_swap(along[k][EARLY:DP])

    along[1], along[-1] = down(along[0]), up(along[0])
    heads_kv, _ = together(key_values, along[0])
    heads_kv = heads_kv.reshape(rows_here, KVH, 2 * HD).swapaxes(0, 1)
    heads_kv = jnp.broadcast_to(heads_kv[:, None], (KVH, NL * NC, rows_here, 2 * HD))
    kv = lax.all_to_all(
        heads_kv.reshape(NZ * NL * NC, rows_here, 2 * HD), tensor, split_axis=0, concat_axis=0, tiled=True
    )
    moved_0 = reduce_y(multiply((0,)))
    along[1], along[-1], kv, *moved_0 = together(along[1], along[-1], kv, *moved_0)
    along[2], along[-2] = down(along[1]), up(along[-1])
    across[1], across[-1] = swap_rest(1), swap_rest(-1)
    total = add(moved_0)
    along[2], along[-2], across[1], across[-1], total = together(along[2], along[-2], across[1], across[-1], total)
    along[3], along[-3] = down(along[2]), up(along[-2])
    across[2], across[-2] = swap_rest(2), swap_rest(-2)
    moved_1 = scatter_y(multiply((1, -1)), iy)
    kv = kv.reshape(seqs, seq_len, 2 * HD).astype(f32)
    along[3], along[-3], across[2], across[-2], kv = together(along[3], along[-3], across[2], across[-2], kv)
    half = along[0].shape[0] // 2
    ends = down(along[3][:half]), up(along[-3][half:])
    across[3], across[-3] = swap_rest(3), swap_rest(-3)
    moved_2 = scatter_y(multiply((2, -2)), iy)
    read = readout.reshape(NZ, NL, NC, rows_here, columns)
    mine = lax.dynamic_index_in_dim(read, ic, 2, False)
    theirs = lax.dynamic_index_in_dim(read, 1 - ic, 2, False)
    *ends, across[3], across[-3], mine, theirs = together(*ends, across[3], across[-3], mine, theirs)
    along[4] = jnp.concatenate(ends)
    across[4] = swap_rest(4)
    moved_3 = reduce_y(multiply((3, -3)))
    read = jnp.concatenate([mine, core_swap(theirs)], axis=-1).astype(f32)
    info = jnp.concatenate([(iz + jnp.array(CHUNKS, jnp.int32) + NZ) % NZ, lengths.reshape(seqs), jnp.stack([il, ic])])
    across[4], info, read = together(across[4], info, read)
    moved_4 = reduce_y(multiply((4,)))
    total = jnp.concatenate([total, moved_1.astype(f32), add(moved_3)])
    cross = hi_swap(total[:, :, 1].astype(bf16))
    cross, total, *moved_4 = together(cross, total, *moved_4)
    early = (total[:, :, 0] + cross.astype(f32)).reshape(-1, 4 * columns)
    last = jnp.concatenate([moved_2.astype(f32), add(moved_4)])
    last = (last[:, :, 0] + hi_swap(last[:, :, 1].astype(bf16)).astype(f32)).reshape(-1, 4 * columns)
    projected = jnp.concatenate([early, last])
    normed_all = jnp.stack(
        [jnp.concatenate([along[k], across[k]]).reshape(NL, DP, rows_here, feats) for k in CHUNKS]
    )
    normed_all = normed_all.transpose(2, 0, 1, 3, 4).reshape(-1, feats)

    grad, tan, sums = attention(info, projected, read, kv)
    spread = jnp.broadcast_to(sums[None], (NZ * NL * NC, 1, LANES))
    spread = lax.all_to_all(spread, tensor, split_axis=0, concat_axis=0, tiled=True).reshape(-1, LANES)
    spread, normed_all = together(spread, normed_all)
    hess_rows = combine(info, ref_margin, spread, grad, tan, seqs).astype(bf16)

    here, there = hess_rows[:, :columns], hess_rows[:, columns:]
    y_gather = lambda v: [v] + [toward("y", NY, dy)(v) for dy in (1, 2, 3)]
    there_x = hi_swap(there)
    here_y = y_gather(here)
    there_x, *here_y = together(there_x, *here_y)
    here_y = jnp.stack(here_y)
    here_all = hi_swap(here_y)
    there_all = y_gather(jnp.stack([there, there_x]))
    here_all, here_y, *there_all = together(here_all, here_y, *there_all)
    hess_all = jnp.concatenate([jnp.stack([here_y, here_all], axis=1), jnp.stack(there_all)], axis=-1)
    outer = lax.dot_general(
        normed_all,
        hess_all.reshape(-1, 2 * columns),
        (((0,), (0,)), ((), ())),
        preferred_element_type=f32,
    )
    return outer[:, :columns] + core_swap(outer[:, columns:].astype(bf16)).astype(f32)


def solution(mesh):
    fine = Mesh(
        mesh.devices.reshape(NY, NX, NZ, NL, NC), ("y", "x_hi", "z", "x_lo", "core")
    )
    dp, tensor = ("y", "x_hi"), ("z", "x_lo", "core")
    return jax.shard_map(
        shards,
        mesh=fine,
        in_specs=(
            P(dp + tensor, None),
            P(),
            P(dp, tensor),
            P(dp, tensor),
            P(dp + tensor, None),
            P(dp, tensor),
            P(dp, None),
            P(dp),
        ),
        out_specs=P(dp, tensor),
        check_vma=False,
    )
```

```python
import functools

import jax
import jax.numpy as jnp
from jax import lax
from jax.experimental import pallas as pl
from jax.experimental.pallas import tpu as pltpu
from jax.sharding import Mesh
from jax.sharding import PartitionSpec as P

HD = 64
KVH = 8
NY, NX, NZ, NL, NC = 4, 2, 8, 2, 2
DP = NY * NX

pair_beta = 0.5
norm_epsilon = 1e-05

bf16 = jnp.bfloat16
f32 = jnp.float32
CHUNKS = (0, 1, -1, 2, -2, 3, -3, 4)
LANES = 128


def toward(axis, size, shift):
    pairs = [((i + shift) % size, i) for i in range(size)]
    return lambda value: lax.ppermute(value, axis, pairs)


core_swap = toward("core", NC, 1)
hi_swap = toward("x_hi", NX, 1)


def together(*values):
    return lax.optimization_barrier(values)


def dot(a, b):
    return jnp.dot(a, b, preferred_element_type=f32)


def reduce_y(partial):
    return [partial[:, 0]] + [toward("y", NY, -dy)(partial[:, dy]) for dy in (2, 1, 3)]


def add(parts):
    total = parts[0].astype(f32)
    for part in parts[1:]:
        total = total + part.astype(f32)
    return total


def attention_kernel(info_ref, both_ref, read_ref, kv_ref, grad_ref, tan_ref, sums_ref, keys_ref, values_ref):
    places, sides, part_rows, columns = read_ref.shape
    seqs = kv_ref.shape[0]
    rows = sides * part_rows
    chunks = both_ref.shape[0] // rows
    pairs = columns // LANES
    per_seq = places // seqs
    scale = f32(HD**-0.5)
    nt = (((1,), (1,)), ((), ()))
    low = lax.broadcasted_iota(jnp.int32, (kv_ref.shape[1], LANES), 1) < HD
    for s in range(seqs):
        kv = kv_ref[s]
        turned = pltpu.roll(kv, HD, 1)
        keys_ref[s] = jnp.concatenate([jnp.where(low, kv, 0.0), jnp.where(low, 0.0, turned)]).astype(bf16)
        values_ref[s] = jnp.concatenate([jnp.where(low, turned, 0.0), jnp.where(low, 0.0, kv)]).astype(bf16)
    lane = lax.broadcasted_iota(jnp.int32, (part_rows, LANES), 1)
    row = lax.broadcasted_iota(jnp.int32, (part_rows, LANES), 0)
    out_lane = lax.broadcasted_iota(jnp.int32, (1, LANES), 1)
    core = info_ref[chunks + seqs]
    stack = lambda blocks: jnp.concatenate(blocks, axis=0)
    column = lambda pair: slice(pair * LANES, (pair + 1) * LANES)
    sums = jnp.zeros((1, LANES), f32)
    for k in range(chunks):
        here = pl.ds(k * rows, rows)
        place = info_ref[k]
        seq = place // per_seq
        length = info_ref[chunks + seq]
        keys, values = keys_ref[seq], values_ref[seq]
        allowed, read = [], []
        for side in range(sides):
            position = ((place % per_seq * sides + side) * NC + core) * part_rows + row
            allowed.append(lane <= jnp.minimum(position, length - 1))
            live = position[:, :1] < length
            read.append(jnp.where(live, read_ref[place, side], 0.0))
        read = stack(read).astype(bf16)
        allowed = stack(allowed * pairs)
        both = both_ref[here, :].astype(bf16)
        both = lax.dot_general(
            stack([both[:, column(p)] for p in range(2 * pairs)]), keys, nt, preferred_element_type=f32
        )
        gain2 = lax.dot_general(
            stack([read[:, column(p)] for p in range(pairs)]), values, nt, preferred_element_type=f32
        )
        scores2, slope2 = both[: pairs * rows] * scale, both[pairs * rows :] * scale
        first, second = [], []
        logp = jnp.zeros((pairs * rows, 1), f32)
        logp_tan = jnp.zeros((pairs * rows, 1), f32)
        for head in range(2):
            part = column(head)
            scores = jnp.where(allowed, scores2[:, part], f32(-1e30))
            slope, gain = slope2[:, part], gain2[:, part]
            weights = jnp.exp(scores - jnp.max(scores, axis=1, keepdims=True))
            probs = weights / jnp.sum(weights, axis=1, keepdims=True)
            mean_gain = jnp.sum(probs * gain, axis=1, keepdims=True)
            mean_slope = jnp.sum(probs * slope, axis=1, keepdims=True)
            lean = gain - mean_gain
            pull = probs * (slope - mean_slope)
            mean_tan = jnp.sum(pull * lean, axis=1, keepdims=True)
            first.append((probs * lean).astype(bf16))
            second.append((pull * lean - probs * mean_tan).astype(bf16))
            logp = logp + mean_gain
            logp_tan = logp_tan + mean_tan
        out = dot(stack([jnp.concatenate(first, axis=1), jnp.concatenate(second, axis=1)]), keys) * scale
        for p in range(pairs):
            grad_ref[here, column(p)] = out[p * rows : (p + 1) * rows]
            tan_ref[here, column(p)] = out[(pairs + p) * rows : (pairs + p + 1) * rows]
        sums = sums + jnp.where(out_lane == seq, jnp.sum(logp), f32(0))
        sums = sums + jnp.where(out_lane == seq + LANES // 2, jnp.sum(logp_tan), f32(0))
    sums_ref[...] = sums


def attention(info, both, read, kv):
    rows, columns = both.shape[0], read.shape[-1]
    vmem = pl.BlockSpec(memory_space=pltpu.VMEM)
    return pl.pallas_call(
        attention_kernel,
        out_shape=(
            jax.ShapeDtypeStruct((rows, columns), f32),
            jax.ShapeDtypeStruct((rows, columns), f32),
            jax.ShapeDtypeStruct((1, LANES), f32),
        ),
        in_specs=[pl.BlockSpec(memory_space=pltpu.SMEM)] + [vmem] * 3,
        out_specs=(vmem, vmem, vmem),
        scratch_shapes=[pltpu.VMEM((kv.shape[0], 2 * kv.shape[1], LANES), bf16)] * 2,
        compiler_params=pltpu.CompilerParams(vmem_limit_bytes=12 * 1024 * 1024),
    )(info, both, read, kv)


def combine_kernel(chunks, seqs, info_ref, margin_ref, spread_ref, grad_ref, tan_ref, out_ref):
    total = jnp.sum(spread_ref[...], axis=0, keepdims=True)
    lane = lax.broadcasted_iota(jnp.int32, (1, LANES), 1)
    at = lambda i: jnp.sum(jnp.where(lane == i, total, f32(0)), axis=1, keepdims=True)
    coeffs = []
    for p in range(seqs // 2):
        margin = pair_beta * (at(2 * p) - at(2 * p + 1) - margin_ref[p])
        margin_tan = pair_beta * (at(LANES // 2 + 2 * p) - at(LANES // 2 + 2 * p + 1))
        sure, unsure = jax.nn.sigmoid(margin), jax.nn.sigmoid(-margin)
        slope = -pair_beta * unsure
        bend = pair_beta * unsure * sure * margin_tan
        coeffs += [(slope, bend), (-slope, -bend)]
    rows = grad_ref.shape[0] // chunks
    per_seq = NZ // seqs
    for k in range(chunks):
        seq = info_ref[k] // per_seq
        coeff, coeff_tan = coeffs[0]
        for s in range(1, seqs):
            coeff = jnp.where(seq == s, coeffs[s][0], coeff)
            coeff_tan = jnp.where(seq == s, coeffs[s][1], coeff_tan)
        here = pl.ds(k * rows, rows)
        out_ref[here, :] = coeff_tan * grad_ref[here, :] + coeff * tan_ref[here, :]


def combine(info, ref_margin, spread, grad, tan, seqs):
    vmem, smem = pl.BlockSpec(memory_space=pltpu.VMEM), pl.BlockSpec(memory_space=pltpu.SMEM)
    return pl.pallas_call(
        functools.partial(combine_kernel, len(CHUNKS), seqs),
        out_shape=jax.ShapeDtypeStruct(grad.shape, f32),
        in_specs=[smem, smem, vmem, vmem, vmem],
        out_specs=vmem,
        compiler_params=pltpu.CompilerParams(vmem_limit_bytes=6 * 1024 * 1024),
    )(info, ref_margin, spread, grad, tan)


def shards(hidden_in, norm_gain, query_weight, probe, key_values, readout, lengths, ref_margin):
    iy, ix, iz, ic = (lax.axis_index(a) for a in ("y", "x_hi", "z", "core"))
    tensor = ("z", "x_lo", "core")
    rows_here, width = hidden_in.shape
    feats, columns = query_weight.shape

    wide = hidden_in.astype(f32)
    stats = jnp.mean(wide * wide, axis=1, keepdims=True)
    normed = (wide * lax.rsqrt(stats + norm_epsilon) * norm_gain.astype(f32)).astype(bf16)

    sides = normed.reshape(rows_here, DP, feats).swapaxes(0, 1)
    sides = jnp.broadcast_to(sides[:, None], (DP, NL, rows_here, feats))
    first = lax.all_to_all(
        sides.reshape(DP * NL, rows_here, feats), ("y", "x_hi", "x_lo"), split_axis=0, concat_axis=0, tiled=True
    )
    weights = jnp.concatenate([query_weight, core_swap(query_weight), probe, core_swap(probe)], axis=1)
    first, weights = together(first, weights)
    first = first.reshape(NY, NX, -1, feats)
    first = lax.dynamic_slice_in_dim(jnp.concatenate([first, first]), iy, NY, 0)
    first = lax.dynamic_slice_in_dim(jnp.concatenate([first, first[:, :1]], axis=1), ix, NX, 1)
    first = first.reshape(DP * NL, rows_here, feats)
    chunk = {}
    (chunk[0],) = together(first)

    seqs = lengths.shape[0] * 2
    seq_len = NZ // seqs * NL * NC * rows_here
    up, down = toward("z", NZ, -1), toward("z", NZ, 1)

    def multiply(group):
        rows = jnp.concatenate([chunk[k] for k in group]).reshape(-1, feats)
        return dot(rows, weights).astype(bf16).reshape(len(group), NY, NX, NL * rows_here, 4 * columns)

    chunk[1], chunk[-1] = down(chunk[0]), up(chunk[0])
    heads_kv, _ = together(key_values, chunk[0])
    heads_kv = heads_kv.reshape(rows_here, KVH, 2 * HD).swapaxes(0, 1)
    heads_kv = jnp.broadcast_to(heads_kv[:, None], (KVH, NL * NC, rows_here, 2 * HD))
    kv = lax.all_to_all(
        heads_kv.reshape(NZ * NL * NC, rows_here, 2 * HD), tensor, split_axis=0, concat_axis=0, tiled=True
    )
    moved_0 = reduce_y(multiply((0,)))
    chunk[1], chunk[-1], kv, *moved_0 = together(chunk[1], chunk[-1], kv, *moved_0)
    chunk[2], chunk[-2] = down(chunk[1]), up(chunk[-1])
    moved_1 = reduce_y(multiply((1, -1)))
    total = add(moved_0)
    chunk[2], chunk[-2], total, *moved_1 = together(chunk[2], chunk[-2], total, *moved_1)
    chunk[3], chunk[-3] = down(chunk[2]), up(chunk[-2])
    moved_2 = reduce_y(multiply((2, -2)))
    total = jnp.concatenate([total, add(moved_1)])
    kv = kv.reshape(seqs, seq_len, 2 * HD).astype(f32)
    read = readout.reshape(NZ, NL, NC, rows_here, columns)
    mine = lax.dynamic_index_in_dim(read, ic, 2, False)
    theirs = lax.dynamic_index_in_dim(read, 1 - ic, 2, False)
    chunk[3], chunk[-3], total, kv, mine, theirs, *moved_2 = together(
        chunk[3], chunk[-3], total, kv, mine, theirs, *moved_2
    )
    half = DP * NL // 2
    ends = down(chunk[3][:half]), up(chunk[-3][half:])
    moved_3 = reduce_y(multiply((3, -3)))
    total = jnp.concatenate([total, add(moved_2)])
    cross = hi_swap(total[:, 1].astype(bf16))
    *ends, total, mine, theirs, _ = together(*ends, total, mine, theirs, moved_3[-1])
    chunk[4] = jnp.concatenate(ends)
    read = jnp.concatenate([mine, core_swap(theirs)], axis=-1).astype(f32)
    info = jnp.concatenate([(iz + jnp.array(CHUNKS, jnp.int32) + NZ) % NZ, lengths.reshape(seqs), ic[None]])
    moved_4 = reduce_y(multiply((4,)))
    cross, total, read, *moved_4 = together(cross, total, read, *moved_4)
    early = (total[:, 0] + cross.astype(f32)).reshape(-1, 4 * columns)
    last = jnp.concatenate([add(moved_3), add(moved_4)])
    last = (last[:, 0] + hi_swap(last[:, 1].astype(bf16)).astype(f32)).reshape(-1, 4 * columns)
    normed_all = jnp.stack([chunk[k].reshape(DP, -1, feats) for k in CHUNKS], axis=1)

    projected = jnp.concatenate([early, last])
    grad, tan, sums = attention(info, projected, read, kv)
    spread = jnp.broadcast_to(sums[None], (NZ * NL * NC, 1, LANES))
    spread = lax.all_to_all(spread, tensor, split_axis=0, concat_axis=0, tiled=True).reshape(-1, LANES)
    spread, normed_all = together(spread, normed_all)
    hess_rows = combine(info, ref_margin, spread, grad, tan, seqs).astype(bf16)

    here, there = hess_rows[:, :columns], hess_rows[:, columns:]
    y_gather = lambda v: [v] + [toward("y", NY, dy)(v) for dy in (1, 2, 3)]
    there_x = hi_swap(there)
    here_y = y_gather(here)
    there_x, *here_y = together(there_x, *here_y)
    here_y = jnp.stack(here_y)
    here_all = hi_swap(here_y)
    there_all = y_gather(jnp.stack([there, there_x]))
    here_all, here_y, *there_all = together(here_all, here_y, *there_all)
    hess_all = jnp.concatenate([jnp.stack([here_y, here_all], axis=1), jnp.stack(there_all)], axis=-1)
    outer = lax.dot_general(
        normed_all.reshape(-1, feats),
        hess_all.reshape(-1, 2 * columns),
        (((0,), (0,)), ((), ())),
        preferred_element_type=f32,
    )
    return outer[:, :columns] + core_swap(outer[:, columns:].astype(bf16)).astype(f32)


def solution(mesh):
    fine = Mesh(
        mesh.devices.reshape(NY, NX, NZ, NL, NC), ("y", "x_hi", "z", "x_lo", "core")
    )
    dp, tensor = ("y", "x_hi"), ("z", "x_lo", "core")
    return jax.shard_map(
        shards,
        mesh=fine,
        in_specs=(
            P(dp + tensor, None),
            P(),
            P(dp, tensor),
            P(dp, tensor),
            P(dp + tensor, None),
            P(dp, tensor),
            P(dp, None),
            P(dp),
        ),
        out_specs=P(dp, tensor),
        check_vma=False,
    )
```

```python
import functools

import jax
import jax.numpy as jnp
from jax import lax
from jax.experimental import pallas as pl
from jax.experimental.pallas import tpu as pltpu
from jax.sharding import Mesh
from jax.sharding import PartitionSpec as P

HD = 64
KVH = 8
NY, NX, NZ, NL, NC = 4, 2, 8, 2, 2
DP = NY * NX

pair_beta = 0.5
norm_epsilon = 1e-05

bf16 = jnp.bfloat16
f32 = jnp.float32
CHUNKS = (0, 1, -1, 2, -2, 3, -3, 4)
LANES = 128


def toward(axis, size, shift):
    pairs = [((i + shift) % size, i) for i in range(size)]
    return lambda value: lax.ppermute(value, axis, pairs)


core_swap = toward("core", NC, 1)
hi_swap = toward("x_hi", NX, 1)


def together(*values):
    return lax.optimization_barrier(values)


def dot(a, b):
    return jnp.dot(a, b, preferred_element_type=f32)


def reduce_y(partial):
    return [partial[:, 0]] + [toward("y", NY, -dy)(partial[:, dy]) for dy in (2, 1, 3)]


def add(parts):
    total = parts[0].astype(f32)
    for part in parts[1:]:
        total = total + part.astype(f32)
    return total


def attention_kernel(info_ref, both_ref, read_ref, kv_ref, grad_ref, tan_ref, sums_ref, keys_ref, values_ref):
    places, sides, part_rows, columns = read_ref.shape
    seqs = kv_ref.shape[0]
    rows = sides * part_rows
    chunks = both_ref.shape[0] // rows
    pairs = columns // LANES
    per_seq = places // seqs
    scale = f32(HD**-0.5)
    nt = (((1,), (1,)), ((), ()))
    low = lax.broadcasted_iota(jnp.int32, (kv_ref.shape[1], LANES), 1) < HD
    for s in range(seqs):
        kv = kv_ref[s]
        turned = pltpu.roll(kv, HD, 1)
        keys_ref[s] = jnp.concatenate([jnp.where(low, kv, 0.0), jnp.where(low, 0.0, turned)]).astype(bf16)
        values_ref[s] = jnp.concatenate([jnp.where(low, turned, 0.0), jnp.where(low, 0.0, kv)]).astype(bf16)
    lane = lax.broadcasted_iota(jnp.int32, (part_rows, LANES), 1)
    row = lax.broadcasted_iota(jnp.int32, (part_rows, LANES), 0)
    out_lane = lax.broadcasted_iota(jnp.int32, (1, LANES), 1)
    core = info_ref[chunks + seqs]
    stack = lambda blocks: jnp.concatenate(blocks, axis=0)
    column = lambda pair: slice(pair * LANES, (pair + 1) * LANES)
    sums = jnp.zeros((1, LANES), f32)
    for k in range(chunks):
        here = pl.ds(k * rows, rows)
        place = info_ref[k]
        seq = place // per_seq
        length = info_ref[chunks + seq]
        keys, values = keys_ref[seq], values_ref[seq]
        allowed, read = [], []
        for side in range(sides):
            position = ((place % per_seq * sides + side) * NC + core) * part_rows + row
            allowed.append(lane <= jnp.minimum(position, length - 1))
            live = position[:, :1] < length
            read.append(jnp.where(live, read_ref[place, side], 0.0))
        read = stack(read).astype(bf16)
        allowed = stack(allowed * pairs)
        both = both_ref[here, :].astype(bf16)
        both = lax.dot_general(
            stack([both[:, column(p)] for p in range(2 * pairs)]), keys, nt, preferred_element_type=f32
        )
        gain2 = lax.dot_general(
            stack([read[:, column(p)] for p in range(pairs)]), values, nt, preferred_element_type=f32
        )
        scores2, slope2 = both[: pairs * rows] * scale, both[pairs * rows :] * scale
        first, second = [], []
        logp = jnp.zeros((pairs * rows, 1), f32)
        logp_tan = jnp.zeros((pairs * rows, 1), f32)
        for head in range(2):
            part = column(head)
            scores = jnp.where(allowed, scores2[:, part], f32(-1e30))
            slope, gain = slope2[:, part], gain2[:, part]
            weights = jnp.exp(scores - jnp.max(scores, axis=1, keepdims=True))
            probs = weights / jnp.sum(weights, axis=1, keepdims=True)
            mean_gain = jnp.sum(probs * gain, axis=1, keepdims=True)
            mean_slope = jnp.sum(probs * slope, axis=1, keepdims=True)
            lean = gain - mean_gain
            pull = probs * (slope - mean_slope)
            mean_tan = jnp.sum(pull * lean, axis=1, keepdims=True)
            first.append((probs * lean).astype(bf16))
            second.append((pull * lean - probs * mean_tan).astype(bf16))
            logp = logp + mean_gain
            logp_tan = logp_tan + mean_tan
        out = dot(stack([jnp.concatenate(first, axis=1), jnp.concatenate(second, axis=1)]), keys) * scale
        for p in range(pairs):
            grad_ref[here, column(p)] = out[p * rows : (p + 1) * rows]
            tan_ref[here, column(p)] = out[(pairs + p) * rows : (pairs + p + 1) * rows]
        sums = sums + jnp.where(out_lane == seq, jnp.sum(logp), f32(0))
        sums = sums + jnp.where(out_lane == seq + LANES // 2, jnp.sum(logp_tan), f32(0))
    sums_ref[...] = sums


def attention(info, both, read, kv):
    rows, columns = both.shape[0], read.shape[-1]
    vmem = pl.BlockSpec(memory_space=pltpu.VMEM)
    return pl.pallas_call(
        attention_kernel,
        out_shape=(
            jax.ShapeDtypeStruct((rows, columns), f32),
            jax.ShapeDtypeStruct((rows, columns), f32),
            jax.ShapeDtypeStruct((1, LANES), f32),
        ),
        in_specs=[pl.BlockSpec(memory_space=pltpu.SMEM)] + [vmem] * 3,
        out_specs=(vmem, vmem, vmem),
        scratch_shapes=[pltpu.VMEM((kv.shape[0], 2 * kv.shape[1], LANES), bf16)] * 2,
        compiler_params=pltpu.CompilerParams(vmem_limit_bytes=12 * 1024 * 1024),
    )(info, both, read, kv)


def combine_kernel(chunks, seqs, info_ref, margin_ref, spread_ref, grad_ref, tan_ref, out_ref):
    total = jnp.sum(spread_ref[...], axis=0, keepdims=True)
    lane = lax.broadcasted_iota(jnp.int32, (1, LANES), 1)
    at = lambda i: jnp.sum(jnp.where(lane == i, total, f32(0)), axis=1, keepdims=True)
    coeffs = []
    for p in range(seqs // 2):
        margin = pair_beta * (at(2 * p) - at(2 * p + 1) - margin_ref[p])
        margin_tan = pair_beta * (at(LANES // 2 + 2 * p) - at(LANES // 2 + 2 * p + 1))
        sure, unsure = jax.nn.sigmoid(margin), jax.nn.sigmoid(-margin)
        slope = -pair_beta * unsure
        bend = pair_beta * unsure * sure * margin_tan
        coeffs += [(slope, bend), (-slope, -bend)]
    rows = grad_ref.shape[0] // chunks
    per_seq = NZ // seqs
    for k in range(chunks):
        seq = info_ref[k] // per_seq
        coeff, coeff_tan = coeffs[0]
        for s in range(1, seqs):
            coeff = jnp.where(seq == s, coeffs[s][0], coeff)
            coeff_tan = jnp.where(seq == s, coeffs[s][1], coeff_tan)
        here = pl.ds(k * rows, rows)
        out_ref[here, :] = coeff_tan * grad_ref[here, :] + coeff * tan_ref[here, :]


def combine(info, ref_margin, spread, grad, tan, seqs):
    vmem, smem = pl.BlockSpec(memory_space=pltpu.VMEM), pl.BlockSpec(memory_space=pltpu.SMEM)
    return pl.pallas_call(
        functools.partial(combine_kernel, len(CHUNKS), seqs),
        out_shape=jax.ShapeDtypeStruct(grad.shape, f32),
        in_specs=[smem, smem, vmem, vmem, vmem],
        out_specs=vmem,
        compiler_params=pltpu.CompilerParams(vmem_limit_bytes=6 * 1024 * 1024),
    )(info, ref_margin, spread, grad, tan)


def shards(hidden_in, norm_gain, query_weight, probe, key_values, readout, lengths, ref_margin):
    iy, ix, iz, ic = (lax.axis_index(a) for a in ("y", "x_hi", "z", "core"))
    tensor = ("z", "x_lo", "core")
    rows_here, width = hidden_in.shape
    feats, columns = query_weight.shape

    wide = hidden_in.astype(f32)
    stats = jnp.mean(wide * wide, axis=1, keepdims=True)
    normed = (wide * lax.rsqrt(stats + norm_epsilon) * norm_gain.astype(f32)).astype(bf16)

    other_q, other_t = core_swap(query_weight), core_swap(probe)
    sides = normed.reshape(rows_here, DP, feats).swapaxes(0, 1)
    sides = jnp.broadcast_to(sides[:, None], (DP, NL, rows_here, feats))
    first = lax.all_to_all(
        sides.reshape(DP * NL, rows_here, feats), ("y", "x_hi", "x_lo"), split_axis=0, concat_axis=0, tiled=True
    )
    first = first.reshape(NY, NX, -1, feats)
    first = lax.dynamic_slice_in_dim(jnp.concatenate([first, first]), iy, NY, 0)
    first = lax.dynamic_slice_in_dim(jnp.concatenate([first, first[:, :1]], axis=1), ix, NX, 1)
    first = first.reshape(DP * NL, rows_here, feats)
    chunk = {}
    chunk[0], other_q, other_t = together(first, other_q, other_t)

    seqs = lengths.shape[0] * 2
    seq_len = NZ // seqs * NL * NC * rows_here
    up, down = toward("z", NZ, -1), toward("z", NZ, 1)

    def multiply(group):
        rows = jnp.concatenate([chunk[k] for k in group]).reshape(-1, feats)
        return dot(rows, weights).astype(bf16).reshape(len(group), NY, NX, NL * rows_here, 4 * columns)

    chunk[1], chunk[-1] = down(chunk[0]), up(chunk[0])
    heads_kv, _ = together(key_values, chunk[0])
    heads_kv = heads_kv.reshape(rows_here, KVH, 2 * HD).swapaxes(0, 1)
    heads_kv = jnp.broadcast_to(heads_kv[:, None], (KVH, NL * NC, rows_here, 2 * HD))
    kv = lax.all_to_all(
        heads_kv.reshape(NZ * NL * NC, rows_here, 2 * HD), tensor, split_axis=0, concat_axis=0, tiled=True
    )
    weights = jnp.concatenate([query_weight, other_q, probe, other_t], axis=1)
    moved_0 = reduce_y(multiply((0,)))
    chunk[1], chunk[-1], kv, weights, *moved_0 = together(chunk[1], chunk[-1], kv, weights, *moved_0)
    chunk[2], chunk[-2] = down(chunk[1]), up(chunk[-1])
    moved_1 = reduce_y(multiply((1, -1)))
    total = add(moved_0)
    chunk[2], chunk[-2], total, *moved_1 = together(chunk[2], chunk[-2], total, *moved_1)
    chunk[3], chunk[-3] = down(chunk[2]), up(chunk[-2])
    moved_2 = reduce_y(multiply((2, -2)))
    total = jnp.concatenate([total, add(moved_1)])
    kv = kv.reshape(seqs, seq_len, 2 * HD).astype(f32)
    read = readout.reshape(NZ, NL, NC, rows_here, columns)
    mine = lax.dynamic_index_in_dim(read, ic, 2, False)
    theirs = lax.dynamic_index_in_dim(read, 1 - ic, 2, False)
    chunk[3], chunk[-3], total, kv, mine, theirs, *moved_2 = together(
        chunk[3], chunk[-3], total, kv, mine, theirs, *moved_2
    )
    half = DP * NL // 2
    ends = down(chunk[3][:half]), up(chunk[-3][half:])
    moved_3 = reduce_y(multiply((3, -3)))
    total = jnp.concatenate([total, add(moved_2)])
    *ends, total, mine, theirs, _ = together(*ends, total, mine, theirs, moved_3[-1])
    chunk[4] = jnp.concatenate(ends)
    read = jnp.concatenate([mine, core_swap(theirs)], axis=-1).astype(f32)
    info = jnp.concatenate([(iz + jnp.array(CHUNKS, jnp.int32) + NZ) % NZ, lengths.reshape(seqs), ic[None]])
    moved_4 = reduce_y(multiply((4,)))
    total = jnp.concatenate([total, add(moved_3)])
    cross = hi_swap(total[:, 1].astype(bf16))
    cross, total, read, *moved_4 = together(cross, total, read, *moved_4)
    last = add(moved_4)
    last = last[:, 0] + hi_swap(last[:, 1].astype(bf16)).astype(f32)
    projected = jnp.concatenate([total[:, 0] + cross.astype(f32), last]).reshape(-1, 4 * columns)
    normed_all = jnp.stack([chunk[k].reshape(DP, -1, feats) for k in CHUNKS], axis=1)

    grad, tan, sums = attention(info, projected, read, kv)
    spread = jnp.broadcast_to(sums[None], (NZ * NL * NC, 1, LANES))
    spread = lax.all_to_all(spread, tensor, split_axis=0, concat_axis=0, tiled=True).reshape(-1, LANES)
    hess_rows = combine(info, ref_margin, spread, grad, tan, seqs).astype(bf16)

    here, there = hess_rows[:, :columns], hess_rows[:, columns:]
    y_gather = lambda v: [v] + [toward("y", NY, dy)(v) for dy in (1, 2, 3)]
    there_x = hi_swap(there)
    here_y = y_gather(here)
    there_x, *here_y = together(there_x, *here_y)
    here_y = jnp.stack(here_y)
    here_all = hi_swap(here_y)
    there_all = y_gather(jnp.stack([there, there_x]))
    here_all, here_y, *there_all = together(here_all, here_y, *there_all)
    hess_all = jnp.concatenate([jnp.stack([here_y, here_all], axis=1), jnp.stack(there_all)], axis=-1)
    left = normed_all.reshape(-1, feats)
    right = hess_all.reshape(-1, 2 * columns)
    outer = lambda b: lax.dot_general(left, b, (((0,), (0,)), ((), ())), preferred_element_type=f32)
    theirs = core_swap(outer(right[:, columns:]).astype(bf16))
    (ours,) = together(outer(right[:, :columns]))
    return ours + theirs.astype(f32)


def solution(mesh):
    fine = Mesh(
        mesh.devices.reshape(NY, NX, NZ, NL, NC), ("y", "x_hi", "z", "x_lo", "core")
    )
    dp, tensor = ("y", "x_hi"), ("z", "x_lo", "core")
    return jax.shard_map(
        shards,
        mesh=fine,
        in_specs=(
            P(dp + tensor, None),
            P(),
            P(dp, tensor),
            P(dp, tensor),
            P(dp + tensor, None),
            P(dp, tensor),
            P(dp, None),
            P(dp),
        ),
        out_specs=P(dp, tensor),
        check_vma=False,
    )
```
